32 devices in a mesh: req: 4 (over y, x), mdl: 8 (over z, core).
Axes of the slice: x: 2, y: 2, z: 4, core: 2. Of those that a mesh axis runs over, the one named last changes fastest.
Arguments:
- tokens: bfloat16 [8192, 1536], P(('req', 'mdl')), may hold values from -3 to 3
- attention_gain: bfloat16 [1536], replicated, may hold values from 0.099609375 to 1.8984375
- feed_gain: bfloat16 [1536], replicated, may hold values from 0.099609375 to 1.8984375
- w_query: bfloat16 [1536, 1536], P('req', 'mdl'), may hold values from -0.4375 to 0.4375
- w_key: bfloat16 [1536, 768], P('req', 'mdl'), may hold values from -0.15625 to 0.15625
- w_value: bfloat16 [1536, 768], P('req', 'mdl'), may hold values from -0.15625 to 0.15625
- w_out: bfloat16 [1536, 1536], P('mdl', 'req'), may hold values from -0.15625 to 0.15625
- w_gate: bfloat16 [1536, 4096], P('req', 'mdl'), may hold values from -0.15625 to 0.15625
- w_up: bfloat16 [1536, 4096], P('req', 'mdl'), may hold values from -0.15625 to 0.15625
- w_down: bfloat16 [4096, 1536], P('mdl', 'req'), may hold values from -0.09375 to 0.09375
- prefix_cache: bfloat16 [2, 4, 4096, 768], P(None, 'req', None, 'mdl'), may hold values from -400 to 400
- lengths: int32 [16], replicated, may hold values from 0 to 512, as said below
- member: int32 [16], replicated, may hold values from 0 to 3
- owners: int32 [4], replicated, may hold values from 0 to 3, as said below
Outputs:
- hidden: bfloat16 [8192, 1536], P(('req', 'mdl'))
- suffix_cache: bfloat16 [2, 8192, 768], P(None, 'req', 'mdl')
The draws below stay inside these ranges and needn't reach their ends.
Inputs may be any that keep to these rules, and one draw needn't show every extreme that they name: `lengths`: some request has 512 live tokens in every draw. Request r reads the prefix of group member[r]. Each slot holds exactly one group: slot owners[g] of prefix_cache holds group g's prefix, whose keys carry rotary encoding at positions 0 to 4095.
All inputs are finite; a program needn't handle non-finite values.
Results may differ from the reference program's by a relative error of at most 0.025.
Values may be sent and summed in bfloat16 or wider, within the bound.
No kernel may reach another device: no remote copies, remote signals or barrier semaphores. Data moves between devices by JAX's collectives and lax.ppermute only.
A program may use at most 128 MiB of HBM per device.

```python
import math
import jax
import jax.numpy as jnp
import numpy as np
from jax import lax

D = 1536
HEADS = 16
KV_HEADS = 8
HD = 96
FF = 4096
PLEN = 4096
SUF = 512
QW = 1536
KVW = 768
GROUPS = 4
REQS = 16
TOKENS = 8192
N_MDL = 8


def draw_prefix_cache(key, part):
    first_key = jax.random.fold_in(jax.random.fold_in(key, 11), 0)
    base = jax.random.normal(first_key, (2, GROUPS, PLEN, KVW), jnp.float32)
    result = jnp.clip(base, -6.0, 6.0)
    return result.astype(jnp.bfloat16)


def draw_lengths(key, part):
    first_key, second_key = jax.random.split(jax.random.fold_in(key, 23), 2)
    base = jax.random.randint(first_key, (REQS,), 0, SUF + 1, dtype=jnp.int32)
    picks = jax.random.permutation(second_key, REQS)
    base = base.at[picks[0]].set(SUF)
    return base.astype(jnp.int32)


def draw_owners(key, part):
    shuffled = jax.random.permutation(jax.random.fold_in(key, 37), GROUPS)
    return shuffled.astype(jnp.int32)


def touch_ends(values, stream_key, low, largest):
    longest = values.shape.index(max(values.shape))
    spots = []
    for shift in (0, 1):
        where = [jax.random.randint(jax.random.fold_in(stream_key, axis), (), 0, length) for axis, length in enumerate(values.shape)]
        where[longest] = (where[longest] + shift) % values.shape[longest]
        spots.append(tuple(where))
    return values.at[spots[0]].set(low).at[spots[1]].set(largest)


def levels(key, extent, pieces, least, largest):
    def one(dim, shards_of):
        heights = jax.random.uniform(jax.random.fold_in(jax.random.fold_in(key, 6), dim), (shards_of,), jnp.float32, least / len(pieces), largest / len(pieces))
        return jnp.repeat(jnp.exp(heights), extent[dim] // shards_of).reshape((-1,) + (1,) * (len(extent) - dim - 1))

    gain = one(*pieces[0])
    for cut in pieces[1:]:
        gain = gain * one(*cut)
    return gain


def rank_bounds(amount, slope):
    loads = [(1 << 20) // math.isqrt(rank ** slope) + 1 for rank in range(1, amount + 1)]
    width = 1 + sum(loads) // (1 << 30)
    return np.cumsum(np.array([max(1, weight // width) for weight in loads]))


def skewed_ids(stream_key, dims, amount, lean):
    grid = rank_bounds(amount, lean)
    pick = jax.random.randint(jax.random.fold_in(stream_key, 1), dims, 0, int(grid[amount - 1]))
    rank = jnp.searchsorted(jnp.asarray(grid, jnp.int32), pick, side="right")
    return jax.random.permutation(jax.random.fold_in(stream_key, 2), amount)[rank].astype(jnp.int32)


def bell_draw(stream_key, shape, scale, most, cuts=(), held_as=jnp.bfloat16):
    loudness = levels(stream_key, shape, cuts, -0.22, 0.18) if cuts else 1.0
    drawn = jax.random.normal(stream_key, shape, jnp.float32) * scale * loudness
    return jnp.minimum(jnp.maximum(drawn, -most), most).astype(held_as)


def setup_inputs(seed: int = 0) -> dict:
    key_list = jax.random.split(jax.random.key(seed), 15)
    return {
        "tokens": bell_draw(key_list[0], (TOKENS, D), 0.5, 3.0, ((0, 32),)),
        "attention_gain": jnp.clip(1.0 + 0.18 * jax.random.normal(key_list[1], (D,), jnp.float32), 0.099609375, 1.8984375).astype(jnp.bfloat16),
        "feed_gain": jnp.clip(1.0 + 0.18 * jax.random.normal(key_list[2], (D,), jnp.float32), 0.099609375, 1.8984375).astype(jnp.bfloat16),
        "w_query": bell_draw(key_list[3], (D, QW), (D // 9) ** -0.5, 0.4375, ((0, 4), (1, 8))),
        "w_key": bell_draw(key_list[4], (D, KVW), D ** -0.5, 0.15625, ((0, 4), (1, 8))),
        "w_value": bell_draw(key_list[5], (D, KVW), D ** -0.5, 0.15625, ((0, 4), (1, 8))),
        "w_out": bell_draw(key_list[6], (QW, D), QW ** -0.5, 0.15625, ((0, 8), (1, 4))),
        "w_gate": bell_draw(key_list[7], (D, FF), D ** -0.5, 0.15625, ((0, 4), (1, 8))),
        "w_up": bell_draw(key_list[8], (D, FF), D ** -0.5, 0.15625, ((0, 4), (1, 8))),
        "w_down": bell_draw(key_list[9], (FF, D), FF ** -0.5, 0.09375, ((0, 8), (1, 4))),
        "prefix_cache": draw_prefix_cache(jax.random.fold_in(key_list[14], 71), 0),
        "lengths": draw_lengths(jax.random.fold_in(key_list[14], 71), 0),
        "member": touch_ends(skewed_ids(key_list[12], (REQS,), GROUPS, 2), jax.random.fold_in(key_list[12], 3), 0, GROUPS - 1).astype(jnp.int32),
        "owners": draw_owners(jax.random.fold_in(key_list[14], 71), 0),
    }


rope_base = 100000.0
norm_eps = 1e-05
far_below = -1e+30

def rms_scale(row_values, norm_gain):
    numbers = row_values.astype(jnp.float32)
    mean_square = lax.optimization_barrier(jnp.mean(numbers * numbers, axis=-1, keepdims=True))
    return numbers * lax.rsqrt(mean_square + norm_eps) * norm_gain.astype(jnp.float32)

def rotate(numbers, positions):
    half_width = numbers.shape[-1] // 2
    frequency = rope_base ** (-(jnp.arange(half_width).astype(jnp.float32) * 2.0 / numbers.shape[-1]))
    angles = positions[:, None] * frequency[None, :]
    cosine = jnp.cos(angles)[:, None, :]
    sine_part = jnp.sin(angles)[:, None, :]
    lower_half = numbers[..., :half_width]
    upper_half = numbers[..., half_width:]
    return jnp.concatenate([lower_half * cosine - upper_half * sine_part, upper_half * cosine + lower_half * sine_part], axis=-1)

def rounded(numbers):
    return lax.optimization_barrier(numbers.astype(jnp.bfloat16)).astype(jnp.float32)

def reference(tokens, attention_gain, feed_gain, w_query, w_key, w_value, w_out, w_gate, w_up, w_down, prefix_cache, lengths, member, owners):
    score_scale = 1.0 / math.sqrt(HD)
    normed = rms_scale(tokens, attention_gain).astype(jnp.bfloat16)
    query_raw = jnp.dot(normed, w_query, preferred_element_type=jnp.float32)
    key_raw = jnp.dot(normed, w_key, preferred_element_type=jnp.float32)
    value_raw = jnp.dot(normed, w_value, preferred_element_type=jnp.float32)
    offsets = jnp.arange(TOKENS, dtype=jnp.int32) % SUF
    positions = (offsets + PLEN).astype(jnp.float32)
    queries = rotate(query_raw.reshape(TOKENS, HEADS, HD), positions).astype(jnp.bfloat16)
    keys = rotate(key_raw.reshape(TOKENS, KV_HEADS, HD), positions).astype(jnp.bfloat16)
    values = value_raw.astype(jnp.bfloat16)
    valid = jnp.arange(SUF, dtype=jnp.int32)[None, :] < lengths[:, None]
    valid_rows = valid.reshape(TOKENS).astype(jnp.float32)
    suffix_cache = (jnp.stack([keys.reshape(TOKENS, KVW).astype(jnp.float32), values.astype(jnp.float32)], 0) * valid_rows[None, :, None]).astype(jnp.bfloat16)
    causal = jnp.arange(SUF)[:, None] >= jnp.arange(SUF)[None, :]

    def attend(request):
        start_row = (request * SUF).astype(jnp.int32)
        query_rows = lax.dynamic_slice_in_dim(queries, start_row, SUF, 0).astype(jnp.float32)
        query_rows = query_rows.reshape(SUF, KV_HEADS, HEADS // KV_HEADS, HD)
        key_rows = lax.dynamic_slice_in_dim(keys, start_row, SUF, 0).astype(jnp.float32)
        value_rows = lax.dynamic_slice_in_dim(values, start_row, SUF, 0).astype(jnp.float32).reshape(SUF, KV_HEADS, HD)
        slot_index = owners[member[request]].astype(jnp.int32)
        prefix_keys = lax.dynamic_index_in_dim(prefix_cache[0], slot_index, 0, keepdims=False).astype(jnp.float32).reshape(PLEN, KV_HEADS, HD)
        prefix_values = lax.dynamic_index_in_dim(prefix_cache[1], slot_index, 0, keepdims=False).astype(jnp.float32).reshape(PLEN, KV_HEADS, HD)
        prefix_scores = jnp.einsum('ikgd,jkd->kgij', query_rows, prefix_keys) * score_scale
        prefix_top = lax.optimization_barrier(jnp.max(prefix_scores, axis=-1))
        prefix_exp = jnp.exp(prefix_scores - prefix_top[..., None])
        prefix_total = lax.optimization_barrier(jnp.sum(prefix_exp, axis=-1))
        prefix_sum = jnp.einsum('kgij,jkd->kgid', rounded(prefix_exp), prefix_values)
        suffix_scores = jnp.einsum('ikgd,jkd->kgij', query_rows, key_rows) * score_scale
        allowed = causal & (jnp.arange(SUF, dtype=jnp.int32)[None, :] < lengths[request])
        masked = jnp.where(allowed, suffix_scores, far_below)
        row_top = jnp.maximum(prefix_top, lax.optimization_barrier(jnp.max(masked, axis=-1)))
        carried = jnp.exp(prefix_top - row_top)
        suffix_exp = jnp.where(allowed, jnp.exp(masked - row_top[..., None]), 0.0)
        row_total = carried * prefix_total + lax.optimization_barrier(jnp.sum(suffix_exp, axis=-1))
        row_sum = carried[..., None] * prefix_sum + jnp.einsum('kgij,jkd->kgid', rounded(suffix_exp), value_rows)
        head_output = (row_sum / row_total[..., None]).astype(jnp.bfloat16)
        return head_output.transpose(2, 0, 1, 3).reshape(SUF, QW)
    attended = lax.map(attend, jnp.arange(REQS, dtype=jnp.int32)).reshape(TOKENS, QW)
    block_width = QW // N_MDL
    attention = jnp.zeros((TOKENS, D), jnp.float32)
    for block in range(N_MDL):
        part_sum = jnp.dot(attended[:, block * block_width:(block + 1) * block_width], w_out[block * block_width:(block + 1) * block_width], preferred_element_type=jnp.float32)
        attention = attention + rounded(part_sum)
    residual = (tokens.astype(jnp.float32) + attention).astype(jnp.bfloat16)
    normed_mid = rms_scale(residual, feed_gain).astype(jnp.bfloat16)
    gate_value = jnp.dot(normed_mid, w_gate, preferred_element_type=jnp.float32)
    up_value = jnp.dot(normed_mid, w_up, preferred_element_type=jnp.float32)
    activation = (jax.nn.silu(gate_value) * up_value).astype(jnp.bfloat16)
    unit_width = FF // N_MDL
    feed = jnp.zeros((TOKENS, D), jnp.float32)
    for block in range(N_MDL):
        part_sum = jnp.dot(activation[:, block * unit_width:(block + 1) * unit_width], w_down[block * unit_width:(block + 1) * unit_width], preferred_element_type=jnp.float32)
        feed = feed + rounded(part_sum)
    hidden = ((residual.astype(jnp.float32) + feed) * valid_rows[:, None]).astype(jnp.bfloat16)
    return (hidden, suffix_cache)
```

```python
import functools
import math

import jax
import jax.numpy as jnp
from jax import lax
from jax.experimental import pallas as pl
from jax.experimental.pallas import tpu as pltpu
from jax.sharding import PartitionSpec as P

HD = 96
SUF = 512


rope_base = 100000.0
norm_eps = 1e-05
far_below = -1e30


def from_partner(block, axis, bit):
    count = lax.axis_size(axis)
    route = []
    for low in range(count):
        high = low | 1 << bit
        if high != low and high < count:
            route += [(low, high), (high, low)]
    return lax.ppermute(block, axis, route)


def rms_scale(row_values, norm_gain):
    numbers = row_values.astype(jnp.float32)
    mean_square = jnp.mean(numbers * numbers, axis=-1, keepdims=True)
    return numbers * lax.rsqrt(mean_square + norm_eps) * norm_gain.astype(jnp.float32)


def rotate(numbers, positions):
    half_width = numbers.shape[-1] // 2
    frequency = rope_base ** (
        -(jnp.arange(half_width).astype(jnp.float32) * 2.0 / numbers.shape[-1])
    )
    angles = positions[:, None] * frequency[None, :]
    cosine = jnp.cos(angles)[:, None, :]
    sine_part = jnp.sin(angles)[:, None, :]
    lower_half = numbers[..., :half_width]
    upper_half = numbers[..., half_width:]
    return jnp.concatenate(
        [
            lower_half * cosine - upper_half * sine_part,
            upper_half * cosine + lower_half * sine_part,
        ],
        axis=-1,
    )


def prefix_part(query_block, key_rows, value_rows, score_scale):
    scores = (
        jnp.einsum("hid,jd->hij", query_block, key_rows, preferred_element_type=jnp.float32)
        * score_scale
    )
    row_top = jnp.max(scores, axis=-1)
    weights = jnp.exp(scores - row_top[..., None])
    row_total = jnp.sum(weights, axis=-1)
    summed = jnp.einsum(
        "hij,jd->hid", weights.astype(jnp.bfloat16), value_rows, preferred_element_type=jnp.float32
    )
    return (row_top, row_total, summed)


def local(
    tokens,
    attention_gain,
    feed_gain,
    w_query,
    w_key,
    w_value,
    w_out,
    w_gate,
    w_up,
    w_down,
    prefix_cache,
    lengths,
    member,
    owners,
):
    w_query, w_key, w_value, w_gate, w_up = (
        lax.all_gather(w_query, "req", axis=0, tiled=True),
        lax.all_gather(w_key, "req", axis=0, tiled=True),
        lax.all_gather(w_value, "req", axis=0, tiled=True),
        lax.all_gather(w_gate, "req", axis=0, tiled=True),
        lax.all_gather(w_up, "req", axis=0, tiled=True),
    )
    w_out, w_down = (
        lax.all_gather(w_out, "req", axis=1, tiled=True),
        lax.all_gather(w_down, "req", axis=1, tiled=True),
    )
    model_devices = lax.axis_size("mdl")
    model_place = lax.axis_index("mdl")
    group_place = lax.axis_index("req")
    local_rows = tokens.shape[0]
    group_rows = local_rows * model_devices
    local_requests = group_rows // SUF
    query_width = w_query.shape[1]
    heads_here = query_width // HD
    pair_width = w_key.shape[1]
    halves = HD // pair_width
    prefix_length = prefix_cache.shape[2]
    score_scale = 1.0 / math.sqrt(HD)
    stacked_weights = jnp.concatenate([w_query, w_key, w_value], axis=1)
    normed = rms_scale(lax.all_gather(tokens, "mdl", axis=0, tiled=True), attention_gain).astype(
        jnp.bfloat16
    )
    projected = jnp.dot(normed, stacked_weights, preferred_element_type=jnp.float32)
    projected_pair = jnp.stack(
        [
            projected[:, query_width : query_width + pair_width],
            projected[:, query_width + pair_width :],
        ],
        axis=0,
    )
    own_prefix = prefix_cache[:, 0]
    low_half = model_place % 2 == 0
    if halves > 1:
        partner = from_partner(projected_pair.astype(jnp.bfloat16), "mdl", 0).astype(
            projected_pair.dtype
        )
        full_pair = jnp.where(
            low_half,
            jnp.concatenate([projected_pair, partner], axis=2),
            jnp.concatenate([partner, projected_pair], axis=2),
        )
        prefix_partner = from_partner(own_prefix, "mdl", 0)
        prefix_full = jnp.where(
            low_half,
            jnp.concatenate([own_prefix, prefix_partner], axis=2),
            jnp.concatenate([prefix_partner, own_prefix], axis=2),
        )
    else:
        full_pair = projected_pair
        prefix_full = own_prefix
    offsets = jnp.arange(group_rows, dtype=jnp.int32) % SUF
    positions = (offsets + prefix_length).astype(jnp.float32)
    queries = rotate(
        projected[:, :query_width].reshape(group_rows, heads_here, HD), positions
    ).astype(jnp.bfloat16)
    keys_rotated = rotate(full_pair[0].reshape(group_rows, 1, HD), positions).reshape(
        group_rows, HD
    )
    key_rows = keys_rotated.astype(jnp.bfloat16)
    value_rows = full_pair[1].astype(jnp.bfloat16)
    local_lengths = lax.dynamic_slice_in_dim(lengths, group_place * local_requests, local_requests)
    valid = jnp.arange(SUF, dtype=jnp.int32)[None, :] < local_lengths[:, None]
    valid_rows = valid.reshape(group_rows)
    own_start = model_place % halves * pair_width
    key_own = lax.dynamic_slice_in_dim(keys_rotated, own_start, pair_width, 1)
    cache_rows = jnp.stack([key_own, projected_pair[1]], axis=0) * valid_rows[None, :, None].astype(
        jnp.float32
    )
    suffix_cache = cache_rows.astype(jnp.bfloat16)
    query_blocks = queries.reshape(local_requests, SUF, heads_here, HD).transpose(0, 2, 1, 3)
    group_numbers = jnp.arange(owners.shape[0], dtype=jnp.int32)
    every_prefix = lax.all_gather(prefix_full[:, None], "req", axis=1, tiled=True)
    local_members = lax.dynamic_slice_in_dim(member, group_place * local_requests, local_requests)
    slot_ids = jnp.sum(
        jnp.where(local_members[:, None] == group_numbers[None, :], owners[None, :], 0), axis=1
    )

    def attend(request):
        slot_index = slot_ids[request]
        prefix_keys = lax.dynamic_index_in_dim(every_prefix[0], slot_index, 0, keepdims=False)
        prefix_values = lax.dynamic_index_in_dim(every_prefix[1], slot_index, 0, keepdims=False)
        return prefix_part(query_blocks[request], prefix_keys, prefix_values, score_scale)

    prefix_top, prefix_total, prefix_sum = lax.map(
        attend, jnp.arange(local_requests, dtype=jnp.int32)
    )
    key_blocks = key_rows.reshape(local_requests, SUF, HD)
    value_blocks = value_rows.reshape(local_requests, SUF, HD)
    scores = (
        jnp.einsum("rhid,rjd->rhij", query_blocks, key_blocks, preferred_element_type=jnp.float32)
        * score_scale
    )
    causal = jnp.arange(SUF)[:, None] >= jnp.arange(SUF)[None, :]
    allowed = (causal[None, :, :] & valid[:, None, :])[:, None]
    masked = jnp.where(allowed, scores, far_below)
    row_top = jnp.maximum(prefix_top, jnp.max(masked, axis=-1))
    carried_share = jnp.exp(prefix_top - row_top)
    weights = jnp.where(allowed, jnp.exp(masked - row_top[..., None]), 0.0)
    row_total = carried_share * prefix_total + jnp.sum(weights, axis=-1)
    summed = carried_share[..., None] * prefix_sum + jnp.einsum(
        "rhij,rjd->rhid",
        weights.astype(jnp.bfloat16),
        value_blocks,
        preferred_element_type=jnp.float32,
    )
    head_output = (summed / row_total[..., None]).astype(jnp.bfloat16)
    attended = head_output.transpose(0, 2, 1, 3).reshape(group_rows, query_width)
    attention_own = lax.psum_scatter(
        jnp.dot(attended, w_out, preferred_element_type=jnp.float32).astype(jnp.bfloat16),
        "mdl",
        scatter_dimension=0,
        tiled=True,
    ).astype(jnp.float32)
    residual = (tokens.astype(jnp.float32) + attention_own).astype(jnp.bfloat16)
    normed_mid = rms_scale(lax.all_gather(residual, "mdl", axis=0, tiled=True), feed_gain).astype(
        jnp.bfloat16
    )
    gate_value = jnp.dot(normed_mid, w_gate, preferred_element_type=jnp.float32)
    up_value = jnp.dot(normed_mid, w_up, preferred_element_type=jnp.float32)
    activation = (jax.nn.silu(gate_value) * up_value).astype(jnp.bfloat16)
    feed_own = lax.psum_scatter(
        jnp.dot(activation, w_down, preferred_element_type=jnp.float32).astype(jnp.bfloat16),
        "mdl",
        scatter_dimension=0,
        tiled=True,
    ).astype(jnp.float32)
    own_valid = lax.dynamic_slice_in_dim(valid_rows, model_place * local_rows, local_rows, 0)
    hidden = (
        (residual.astype(jnp.float32) + feed_own) * own_valid[:, None].astype(jnp.float32)
    ).astype(jnp.bfloat16)
    return (hidden, suffix_cache)


def any_specs(count):
    return [pl.BlockSpec(memory_space=pl.ANY)] * count


def device_call(kernel, outputs, in_specs, scratch, flops, moved):
    return pl.pallas_call(
        kernel,
        out_shape=outputs,
        grid_spec=pltpu.PrefetchScalarGridSpec(
            num_scalar_prefetch=1,
            grid=(1,),
            in_specs=in_specs,
            out_specs=jax.tree.map(
                lambda out: pl.BlockSpec(out.shape, lambda *_: (0,) * len(out.shape)), outputs
            ),
            scratch_shapes=scratch,
        ),
        compiler_params=pltpu.CompilerParams(vmem_limit_bytes=48 * 1024 * 1024),
        cost_estimate=pl.CostEstimate(
            flops=int(flops), bytes_accessed=int(moved), transcendentals=0
        ),
    )


def whole_spec(array):
    return pl.BlockSpec(array.shape, lambda *_: (0,) * array.ndim)


def across_first(index, count):
    return [(place, place ^ index) for place in range(count)]


def dot_rows(left, right):
    return lax.dot_general(left, right, (((1,), (1,)), ((), ())), preferred_element_type=jnp.float32)


def square_first(block):
    return (
        lax.ppermute(block, "req", across_first(1, 4)),
        lax.ppermute(block, "req", across_first(2, 4)),
    )


def square_second(beside, above):
    half = beside.shape[0] // 2
    return (
        lax.ppermute(above[:half], "req", across_first(1, 4)),
        lax.ppermute(beside[half:], "req", across_first(2, 4)),
    )


def project_kernel(lines, offsets, idx, *refs):
    count = len(offsets)
    row_refs, weight_refs = refs[:count], refs[count : count + 5]
    cosine_ref, sine_ref, query_ref, cache_ref, rows, weights, row_sems, weight_sems = refs[
        count + 5 :
    ]
    line, core, square = idx[0], idx[1], idx[2]
    block = row_refs[0].shape[0]
    depth = weight_refs[0].shape[1]
    half_out = weight_refs[3].shape[0]
    full_out = weight_refs[0].shape[0]

    def weight_copies():
        copies = []
        for number, (flip, start, size) in enumerate(
            [(0, 0, full_out), (1, 0, full_out), (2, 0, full_out), (3, 0, half_out), (3, half_out, half_out)]
        ):
            columns = pl.ds(pl.multiple_of((square ^ flip) * depth, 128), depth)
            copies.append(
                pltpu.make_async_copy(
                    weight_refs[number],
                    weights.at[pl.ds(start, size), columns],
                    weight_sems.at[number],
                )
            )
        return copies

    def row_copy(number):
        offset, flip = offsets[number]
        place = (line + offset) * 2 + (core ^ flip)
        return pltpu.make_async_copy(
            row_refs[number],
            rows.at[pl.ds(pl.multiple_of(place * block, 16), block), :],
            row_sems.at[number],
        )

    def present(number):
        there = line + offsets[number][0]
        return jnp.logical_and(there >= 0, there < lines)

    for copy in weight_copies():
        copy.start()
    for number in range(count):
        pl.when(present(number))(lambda number=number: row_copy(number).start())
    for copy in weight_copies():
        copy.wait()
    for number in range(count):
        pl.when(present(number))(lambda number=number: row_copy(number).wait())
    half = HD // 2

    @pl.loop(0, 2 * lines)
    def _(step):
        here = pl.ds(pl.multiple_of(step * block, 128), block)
        within = lax.rem(step, 2) * block
        columns = pl.ds(pl.multiple_of(within, 128), block)
        projected = dot_rows(weights[...], rows[here, :])
        cosine, sine = cosine_ref[:, columns], sine_ref[:, columns]

        def turned(start):
            lower, upper = projected[start : start + half], projected[start + half : start + HD]
            return jnp.concatenate(
                [lower * cosine - upper * sine, upper * cosine + lower * sine], axis=0
            )

        for head in range(2):
            query_ref[head, here, :] = turned(head * HD).T.astype(jnp.bfloat16)
        live = (
            within + lax.broadcasted_iota(jnp.int32, (HD, block), 1) < idx[3 + lax.div(step, 2)]
        )
        cache_ref[0, :, here] = jnp.where(live, turned(2 * HD), 0.0).astype(jnp.bfloat16)
        cache_ref[1, :, here] = jnp.where(live, projected[3 * HD :], 0.0).astype(jnp.bfloat16)


def attend_kernel(
    idx,
    query_all,
    cache_all,
    own,
    beside,
    above,
    far_key,
    far_value,
    same_ref,
    other_ref,
    queries,
    suffix,
    key_buf,
    value_buf,
    value_rows,
    sems,
):
    request, source, length, core = idx[0], idx[1], idx[2], idx[3]
    plen = key_buf.shape[1]
    tail = suffix.shape[2]
    place = pl.ds(pl.multiple_of(request * tail, 128), tail)
    copies = [
        pltpu.make_async_copy(query_all.at[:, place, :], queries, sems.at[0]),
        pltpu.make_async_copy(cache_all.at[:, :, place], suffix, sems.at[1]),
    ]
    for copy in copies:
        copy.start()
    keys = [own.at[0], beside.at[0], above.at[0], far_key.at[0]]
    values = [own.at[1], beside.at[1], above.at[1], far_value.at[0]]
    for number in range(4):

        @pl.when(source == number)
        def _(number=number):
            pltpu.make_async_copy(keys[number], key_buf, sems.at[2]).start()
            pltpu.make_async_copy(values[number], value_buf, sems.at[3]).start()

    for copy in copies:
        copy.wait()
    pltpu.make_async_copy(keys[0], key_buf, sems.at[2]).wait()
    pltpu.make_async_copy(values[0], value_buf, sems.at[3]).wait()

    def with_ones(piece):
        lanes = piece.shape[1]
        marks = (lax.broadcasted_iota(jnp.int32, (128 - HD, lanes), 0) == 0).astype(jnp.float32)
        return jnp.concatenate([piece.astype(jnp.float32), marks], axis=0).T.astype(jnp.bfloat16)

    step = 512

    @pl.loop(0, plen // step)
    def _(part):
        here = pl.ds(pl.multiple_of(part * step, 128), step)
        value_rows[here, :] = with_ones(value_buf[:, here])

    value_rows[pl.ds(plen, tail), :] = with_ones(suffix[1])
    factor = math.log2(math.e) / math.sqrt(HD)
    rows = 128
    chunk = 1024

    def one_block(start, out_ref, out_start):
        pair = jnp.concatenate(
            [queries[0, pl.ds(start, rows), :], queries[1, pl.ds(start, rows), :]], axis=0
        )
        top, total = None, None
        for part in range(plen // chunk + 1):
            if part < plen // chunk:
                scores = jnp.dot(
                    pair,
                    key_buf[:, part * chunk : (part + 1) * chunk],
                    preferred_element_type=jnp.float32,
                )
                held = value_rows[part * chunk : (part + 1) * chunk, :]
            else:
                scores = jnp.dot(pair, suffix[0], preferred_element_type=jnp.float32)
                row = lax.broadcasted_iota(jnp.int32, scores.shape, 0)
                row = start + jnp.where(row >= rows, row - rows, row)
                column = lax.broadcasted_iota(jnp.int32, scores.shape, 1)
                allowed = jnp.logical_and(column <= row, column < length)
                scores = jnp.where(allowed, scores, far_below)
                held = value_rows[plen:, :]
            highest = jnp.max(scores, axis=1, keepdims=True)
            new_top = highest if top is None else jnp.maximum(top, highest)
            weights = jnp.exp2((scores - new_top) * factor).astype(jnp.bfloat16)
            added = jnp.dot(weights, held, preferred_element_type=jnp.float32)
            total = (
                added if total is None else total * jnp.exp2((top - new_top) * factor) + added
            )
            top = new_top
        result = (total[:, :HD] / total[:, HD : HD + 1]).astype(jnp.bfloat16)
        out_ref[pl.ds(out_start, rows), :] = jnp.concatenate([result[:rows], result[rows:]], axis=1)

    halves = tail // 2
    for flip, out_ref in enumerate((same_ref, other_ref)):

        @pl.loop(0, halves // rows)
        def _(part, flip=flip, out_ref=out_ref):
            out_start = pl.multiple_of(part * rows, rows)
            start = pl.multiple_of((core ^ flip) * halves + out_start, rows)

            @pl.when(start < length)
            def _():
                one_block(start, out_ref, out_start)

            @pl.when(start >= length)
            def _():
                out_ref[pl.ds(out_start, rows), :] = jnp.zeros((rows, 2 * HD), jnp.bfloat16)


def output_kernel(lines, idx, *refs):
    pieces = refs[: 2 * lines]
    weight, tokens, gain, residual_ref, normed_ref = refs[2 * lines :]
    line, core = idx[0], idx[1]
    width = pieces[0].shape[1]
    total = jnp.zeros(tokens.shape, jnp.float32)
    for number, piece in enumerate(pieces):
        shift, flip = number // 2, number % 2
        place = lax.rem(line + lines - shift, lines) * 2 + (core ^ flip)
        total += jnp.dot(
            piece[...],
            weight[pl.ds(pl.multiple_of(place * width, 16), width), :],
            preferred_element_type=jnp.float32,
        )
    residual = (tokens[...].astype(jnp.float32) + total).astype(jnp.bfloat16)
    residual_ref[...] = residual
    numbers = residual.astype(jnp.float32)
    mean_square = jnp.mean(numbers * numbers, axis=-1, keepdims=True)
    normed_ref[...] = (
        numbers * lax.rsqrt(mean_square + norm_eps) * gain[...].astype(jnp.float32)
    ).astype(jnp.bfloat16)


def gather_pieces(refs, square, full, split):
    if len(refs) == 1:
        return [(refs[0].at[pl.ds(place * full, full), :], place, 0, full) for place in range(4)]
    return [
        (refs[0], square, 0, full),
        (refs[1], square ^ 1, 0, full),
        (refs[2], square ^ 2, 0, full),
        (refs[3], square ^ 3, 0, split),
        (refs[4], square ^ 3, split, full - split),
    ]


def activate_kernel(weight_count, row_count, idx, *refs):
    weight_refs = refs[:weight_count]
    row_refs = refs[weight_count : weight_count + row_count]
    out_ref, gate, up, sems = refs[weight_count + row_count :]
    square = idx[2]
    depth = gate.shape[0] // 4
    copies = []
    for source, place, first, size in gather_pieces(weight_refs, square, 2 * depth, depth):
        target = pl.ds(pl.multiple_of(place * depth, 128), depth)
        if first == 0:
            copies.append((source.at[pl.ds(0, depth), :], gate.at[target, :]))
        if first + size == 2 * depth:
            copies.append((source.at[pl.ds(size - depth, depth), :], up.at[target, :]))
    copies = [
        pltpu.make_async_copy(source, target, sems.at[number])
        for number, (source, target) in enumerate(copies)
    ]
    for copy in copies:
        copy.start()
    for copy in copies:
        copy.wait()
    block = row_refs[0].shape[0]
    for number, row_ref in enumerate(row_refs):
        rows = row_ref[...]
        gated = jnp.dot(rows, gate[...], preferred_element_type=jnp.float32)
        upper = jnp.dot(rows, up[...], preferred_element_type=jnp.float32)
        out_ref[number * block : (number + 1) * block, :] = (
            gated / (1.0 + jnp.exp(-gated)) * upper
        ).astype(jnp.bfloat16)


def down_kernel(counts, block, idx, *refs):
    first_refs, refs = refs[: counts[0]], refs[counts[0] :]
    second_refs, refs = refs[: counts[1]], refs[counts[1] :]
    first_act, second_act, out_a, out_b, first, second, sems = refs
    square = idx[2]
    hidden, width = first.shape[0], first.shape[1] // 4
    copies = []
    for held, target in ((first_refs, first), (second_refs, second)):
        for source, place, start, size in gather_pieces(held, square, hidden, hidden // 2):
            columns = pl.ds(pl.multiple_of(place * width, 128), width)
            copies.append((source, target.at[pl.ds(start, size), columns]))
    copies = [
        pltpu.make_async_copy(source, target, sems.at[number])
        for number, (source, target) in enumerate(copies)
    ]
    for copy in copies:
        copy.start()
    for copy in copies:
        copy.wait()
    for number, out_ref in enumerate((out_a, out_b)):
        here = slice(number * block, (number + 1) * block)
        out_ref[...] = (
            jnp.dot(first_act[here], first[...], preferred_element_type=jnp.float32)
            + jnp.dot(second_act[here], second[...], preferred_element_type=jnp.float32)
        ).astype(jnp.bfloat16)


def square_local(
    tokens,
    attention_gain,
    feed_gain,
    w_query,
    w_key,
    w_value,
    w_out,
    w_gate,
    w_up,
    w_down,
    prefix_cache,
    lengths,
    member,
    owners,
):
    model_devices = lax.axis_size("mdl")
    lines = model_devices // 2
    place = lax.axis_index("mdl")
    square = lax.axis_index("req")
    line, core = place // 2, place % 2
    block, width = tokens.shape
    group_rows = block * model_devices
    hidden = w_gate.shape[1]
    plen = prefix_cache.shape[2]
    bf16 = jnp.bfloat16

    def to_core(array):
        return lax.ppermute(array, "mdl", across_first(1, model_devices))

    def along(array, step, first=0):
        route = []
        for spot in range(lines):
            began = spot - first if step > 0 else spot + first
            if 0 <= spot + step < lines and 0 <= began < lines:
                route += [(2 * spot + side, 2 * (spot + step) + side) for side in range(2)]
        return lax.ppermute(array, "mdl", route)

    def shifted(array, step, flip):
        route = []
        for spot in range(lines):
            for side in range(2):
                route.append((2 * spot + side, 2 * ((spot + step) % lines) + (side ^ flip)))
        return lax.ppermute(array, "mdl", route)

    local_lengths = lax.dynamic_slice_in_dim(lengths, square * lines, lines)
    local_members = lax.dynamic_slice_in_dim(member, square * lines, lines)
    group_numbers = jnp.arange(owners.shape[0], dtype=jnp.int32)
    slot_ids = jnp.sum(
        jnp.where(local_members[:, None] == group_numbers[None, :], owners[None, :], 0), axis=1
    )
    sources = slot_ids ^ square
    where_am_i = jnp.concatenate([jnp.stack([line, core, square]), local_lengths]).astype(jnp.int32)

    projection = jnp.concatenate([w_query.T, w_key.T, w_value.T], axis=0)
    projection_beside, projection_above = square_first(projection)
    prefix = jnp.swapaxes(prefix_cache[:, 0], 1, 2)
    prefix_beside, prefix_above = square_first(prefix)
    projection_far = square_second(projection_beside, projection_above)

    normed = rms_scale(tokens, attention_gain).astype(bf16)
    arrived, offsets = [normed, to_core(normed)], [(0, 0), (0, 1)]
    upward, downward = normed, normed
    for step in range(1, lines):
        upward, downward = along(upward, 1, step - 1), along(downward, -1, step - 1)
        arrived += [upward, to_core(upward), downward, to_core(downward)]
        offsets += [(-step, 0), (-step, 1), (step, 0), (step, 1)]

    half = HD // 2
    frequency = rope_base ** (-(jnp.arange(half).astype(jnp.float32) * 2.0 / HD))
    positions = (jnp.arange(SUF, dtype=jnp.int32) + plen).astype(jnp.float32)
    angles = frequency[:, None] * positions[None, :]
    cosine, sine = jnp.cos(angles), jnp.sin(angles)
    outputs = (
        jax.ShapeDtypeStruct((2, group_rows, HD), bf16),
        jax.ShapeDtypeStruct((2, HD, group_rows), bf16),
    )
    queries, cache = device_call(
        functools.partial(project_kernel, lines, offsets),
        outputs,
        any_specs(len(arrived) + 5) + [whole_spec(cosine), whole_spec(sine)],
        [
            pltpu.VMEM((group_rows, width), bf16),
            pltpu.VMEM((4 * HD, width), bf16),
            pltpu.SemaphoreType.DMA((len(arrived),)),
            pltpu.SemaphoreType.DMA((5,)),
        ],
        2 * group_rows * width * 4 * HD,
        2 * group_rows * width,
    )(
        where_am_i,
        *arrived,
        projection,
        projection_beside,
        projection_above,
        *projection_far,
        cosine,
        sine,
    )
    prefix_far = square_second(prefix_beside, prefix_above)

    gate_up = jnp.concatenate([w_gate, w_up], axis=0)
    gate_up_z = lax.ppermute(gate_up, "mdl", across_first(4, model_devices))
    down_z = lax.ppermute(w_down, "mdl", across_first(4, model_devices))
    late_gate_up, late_down, _ = lax.optimization_barrier((gate_up, w_down, prefix_beside))
    first_gate_up = [lax.all_gather(late_gate_up, "req", axis=0, tiled=True)]
    first_down = [lax.all_gather(late_down, "req", axis=0, tiled=True)]
    gate_up_z, down_z, _ = lax.optimization_barrier((gate_up_z, down_z, prefix_far))
    gate_up_beside, gate_up_above = square_first(gate_up_z)
    down_beside, down_above = square_first(down_z)
    second_gate_up = [
        gate_up_z,
        gate_up_beside,
        gate_up_above,
        *square_second(gate_up_beside, gate_up_above),
    ]
    second_down = [down_z, down_beside, down_above, *square_second(down_beside, down_above)]
    out_rows = lax.all_gather(w_out, "req", axis=1, tiled=True)
    out_weight = lax.all_gather(out_rows, "mdl", axis=0, tiled=True)

    pieces = {}
    for shift in [*range(lines // 2, 0, -1), *range(lines // 2 + 1, lines), 0]:
        request = (line + shift) % lines
        facts = jnp.stack(
            [
                request,
                lax.dynamic_index_in_dim(sources, request, 0, False),
                lax.dynamic_index_in_dim(local_lengths, request, 0, False),
                core,
            ]
        ).astype(jnp.int32)
        same, other = device_call(
            attend_kernel,
            (jax.ShapeDtypeStruct((SUF // 2, 2 * HD), bf16),) * 2,
            any_specs(7),
            [
                pltpu.VMEM((2, SUF, HD), bf16),
                pltpu.VMEM((2, HD, SUF), bf16),
                pltpu.VMEM((HD, plen), bf16),
                pltpu.VMEM((HD, plen), bf16),
                pltpu.VMEM((plen + SUF, 128), bf16),
                pltpu.SemaphoreType.DMA((4,)),
            ],
            4 * 2 * SUF * plen * 256,
            4 * plen * HD,
        )(facts, queries, cache, prefix, prefix_beside, prefix_above, *prefix_far)
        if shift:
            pieces[shift] = (shifted(same, shift, 0), shifted(other, shift, 1))
        else:
            pieces[shift] = (same, to_core(other))
    attended = [piece for shift in range(lines) for piece in pieces[shift]]
    residual, normed_mid = device_call(
        functools.partial(output_kernel, lines),
        (jax.ShapeDtypeStruct((block, width), bf16),) * 2,
        [whole_spec(piece) for piece in attended]
        + [whole_spec(out_weight), whole_spec(tokens), pl.BlockSpec((1, width), lambda *_: (0, 0))],
        [],
        2 * block * width * width,
        2 * width * width,
    )(where_am_i, *attended, out_weight, tokens, feed_gain[None, :])

    def to_neighbour(array):
        return lax.ppermute(array, "mdl", across_first(2, model_devices))

    far_rows = to_neighbour(normed_mid)
    own_rows = [normed_mid, to_core(normed_mid)]
    far_rows = [far_rows, to_core(far_rows)]

    def activate(weights, rows):
        return device_call(
            functools.partial(activate_kernel, len(weights), len(rows)),
            jax.ShapeDtypeStruct((len(rows) * block, hidden), bf16),
            any_specs(len(weights)) + [whole_spec(row) for row in rows],
            [
                pltpu.VMEM((width, hidden), bf16),
                pltpu.VMEM((width, hidden), bf16),
                pltpu.SemaphoreType.DMA((8,)),
            ],
            4 * len(rows) * block * width * hidden,
            4 * width * hidden,
        )(where_am_i, *weights, *rows)

    first_own = activate(first_gate_up, own_rows)
    first_far = activate(first_gate_up, far_rows)
    second_both = activate(second_gate_up, [*far_rows, *own_rows])

    def down(first_act, part):
        return device_call(
            functools.partial(down_kernel, (len(first_down), len(second_down)), block),
            (jax.ShapeDtypeStruct((block, width), bf16),) * 2,
            any_specs(len(first_down) + len(second_down))
            + [
                whole_spec(first_act),
                pl.BlockSpec((2 * block, hidden), lambda *_, part=part: (part, 0)),
            ],
            [
                pltpu.VMEM((hidden, width), bf16),
                pltpu.VMEM((hidden, width), bf16),
                pltpu.SemaphoreType.DMA((9,)),
            ],
            8 * block * width * hidden,
            4 * width * hidden,
        )(where_am_i, *first_down, *second_down, first_act, second_both)

    def added(left, right):
        return left.astype(jnp.float32) + right.astype(jnp.float32)

    far_sum, far_core = down(first_far, 0)
    far_sum = to_neighbour(added(far_sum, to_core(far_core)).astype(bf16))
    own_sum, own_core = down(first_own, 1)
    feed = added(own_sum, to_core(own_core)) + far_sum.astype(jnp.float32)
    live = core * block + jnp.arange(block, dtype=jnp.int32) < lax.dynamic_index_in_dim(
        local_lengths, line, 0, False
    )
    result = jnp.where(live[:, None], residual.astype(jnp.float32) + feed, 0.0).astype(bf16)
    return (result, jnp.swapaxes(cache, 1, 2))


def solution(mesh):
    placed = (
        P(("req", "mdl"), None),
        P(),
        P(),
        P("req", "mdl"),
        P("req", "mdl"),
        P("req", "mdl"),
        P("mdl", "req"),
        P("req", "mdl"),
        P("req", "mdl"),
        P("mdl", "req"),
        P(None, "req", None, "mdl"),
        P(),
        P(),
        P(),
    )
    square = mesh.shape["req"] == 4 and mesh.shape["mdl"] == 8
    return jax.shard_map(
        square_local if square else local,
        mesh=mesh,
        in_specs=placed,
        out_specs=(P(("req", "mdl"), None), P(None, "req", "mdl")),
        check_vma=False,
    )
```

```python
import functools
import math

import jax
import jax.numpy as jnp
from jax import lax
from jax.experimental import pallas as pl
from jax.experimental.pallas import tpu as pltpu
from jax.sharding import PartitionSpec as P

HD = 96
SUF = 512


rope_base = 100000.0
norm_eps = 1e-05
far_below = -1e30


def from_partner(block, axis, bit):
    count = lax.axis_size(axis)
    route = []
    for low in range(count):
        high = low | 1 << bit
        if high != low and high < count:
            route += [(low, high), (high, low)]
    return lax.ppermute(block, axis, route)


def rms_scale(row_values, norm_gain):
    numbers = row_values.astype(jnp.float32)
    mean_square = jnp.mean(numbers * numbers, axis=-1, keepdims=True)
    return numbers * lax.rsqrt(mean_square + norm_eps) * norm_gain.astype(jnp.float32)


def rotate(numbers, positions):
    half_width = numbers.shape[-1] // 2
    frequency = rope_base ** (
        -(jnp.arange(half_width).astype(jnp.float32) * 2.0 / numbers.shape[-1])
    )
    angles = positions[:, None] * frequency[None, :]
    cosine = jnp.cos(angles)[:, None, :]
    sine_part = jnp.sin(angles)[:, None, :]
    lower_half = numbers[..., :half_width]
    upper_half = numbers[..., half_width:]
    return jnp.concatenate(
        [
            lower_half * cosine - upper_half * sine_part,
            upper_half * cosine + lower_half * sine_part,
        ],
        axis=-1,
    )


def prefix_part(query_block, key_rows, value_rows, score_scale):
    scores = (
        jnp.einsum("hid,jd->hij", query_block, key_rows, preferred_element_type=jnp.float32)
        * score_scale
    )
    row_top = jnp.max(scores, axis=-1)
    weights = jnp.exp(scores - row_top[..., None])
    row_total = jnp.sum(weights, axis=-1)
    summed = jnp.einsum(
        "hij,jd->hid", weights.astype(jnp.bfloat16), value_rows, preferred_element_type=jnp.float32
    )
    return (row_top, row_total, summed)


def local(
    tokens,
    attention_gain,
    feed_gain,
    w_query,
    w_key,
    w_value,
    w_out,
    w_gate,
    w_up,
    w_down,
    prefix_cache,
    lengths,
    member,
    owners,
):
    w_query, w_key, w_value, w_gate, w_up = (
        lax.all_gather(w_query, "req", axis=0, tiled=True),
        lax.all_gather(w_key, "req", axis=0, tiled=True),
        lax.all_gather(w_value, "req", axis=0, tiled=True),
        lax.all_gather(w_gate, "req", axis=0, tiled=True),
        lax.all_gather(w_up, "req", axis=0, tiled=True),
    )
    w_out, w_down = (
        lax.all_gather(w_out, "req", axis=1, tiled=True),
        lax.all_gather(w_down, "req", axis=1, tiled=True),
    )
    model_devices = lax.axis_size("mdl")
    model_place = lax.axis_index("mdl")
    group_place = lax.axis_index("req")
    local_rows = tokens.shape[0]
    group_rows = local_rows * model_devices
    local_requests = group_rows // SUF
    query_width = w_query.shape[1]
    heads_here = query_width // HD
    pair_width = w_key.shape[1]
    halves = HD // pair_width
    prefix_length = prefix_cache.shape[2]
    score_scale = 1.0 / math.sqrt(HD)
    stacked_weights = jnp.concatenate([w_query, w_key, w_value], axis=1)
    normed = rms_scale(lax.all_gather(tokens, "mdl", axis=0, tiled=True), attention_gain).astype(
        jnp.bfloat16
    )
    projected = jnp.dot(normed, stacked_weights, preferred_element_type=jnp.float32)
    projected_pair = jnp.stack(
        [
            projected[:, query_width : query_width + pair_width],
            projected[:, query_width + pair_width :],
        ],
        axis=0,
    )
    own_prefix = prefix_cache[:, 0]
    low_half = model_place % 2 == 0
    if halves > 1:
        partner = from_partner(projected_pair.astype(jnp.bfloat16), "mdl", 0).astype(
            projected_pair.dtype
        )
        full_pair = jnp.where(
            low_half,
            jnp.concatenate([projected_pair, partner], axis=2),
            jnp.concatenate([partner, projected_pair], axis=2),
        )
        prefix_partner = from_partner(own_prefix, "mdl", 0)
        prefix_full = jnp.where(
            low_half,
            jnp.concatenate([own_prefix, prefix_partner], axis=2),
            jnp.concatenate([prefix_partner, own_prefix], axis=2),
        )
    else:
        full_pair = projected_pair
        prefix_full = own_prefix
    offsets = jnp.arange(group_rows, dtype=jnp.int32) % SUF
    positions = (offsets + prefix_length).astype(jnp.float32)
    queries = rotate(
        projected[:, :query_width].reshape(group_rows, heads_here, HD), positions
    ).astype(jnp.bfloat16)
    keys_rotated = rotate(full_pair[0].reshape(group_rows, 1, HD), positions).reshape(
        group_rows, HD
    )
    key_rows = keys_rotated.astype(jnp.bfloat16)
    value_rows = full_pair[1].astype(jnp.bfloat16)
    local_lengths = lax.dynamic_slice_in_dim(lengths, group_place * local_requests, local_requests)
    valid = jnp.arange(SUF, dtype=jnp.int32)[None, :] < local_lengths[:, None]
    valid_rows = valid.reshape(group_rows)
    own_start = model_place % halves * pair_width
    key_own = lax.dynamic_slice_in_dim(keys_rotated, own_start, pair_width, 1)
    cache_rows = jnp.stack([key_own, projected_pair[1]], axis=0) * valid_rows[None, :, None].astype(
        jnp.float32
    )
    suffix_cache = cache_rows.astype(jnp.bfloat16)
    query_blocks = queries.reshape(local_requests, SUF, heads_here, HD).transpose(0, 2, 1, 3)
    group_numbers = jnp.arange(owners.shape[0], dtype=jnp.int32)
    every_prefix = lax.all_gather(prefix_full[:, None], "req", axis=1, tiled=True)
    local_members = lax.dynamic_slice_in_dim(member, group_place * local_requests, local_requests)
    slot_ids = jnp.sum(
        jnp.where(local_members[:, None] == group_numbers[None, :], owners[None, :], 0), axis=1
    )

    def attend(request):
        slot_index = slot_ids[request]
        prefix_keys = lax.dynamic_index_in_dim(every_prefix[0], slot_index, 0, keepdims=False)
        prefix_values = lax.dynamic_index_in_dim(every_prefix[1], slot_index, 0, keepdims=False)
        return prefix_part(query_blocks[request], prefix_keys, prefix_values, score_scale)

    prefix_top, prefix_total, prefix_sum = lax.map(
        attend, jnp.arange(local_requests, dtype=jnp.int32)
    )
    key_blocks = key_rows.reshape(local_requests, SUF, HD)
    value_blocks = value_rows.reshape(local_requests, SUF, HD)
    scores = (
        jnp.einsum("rhid,rjd->rhij", query_blocks, key_blocks, preferred_element_type=jnp.float32)
        * score_scale
    )
    causal = jnp.arange(SUF)[:, None] >= jnp.arange(SUF)[None, :]
    allowed = (causal[None, :, :] & valid[:, None, :])[:, None]
    masked = jnp.where(allowed, scores, far_below)
    row_top = jnp.maximum(prefix_top, jnp.max(masked, axis=-1))
    carried_share = jnp.exp(prefix_top - row_top)
    weights = jnp.where(allowed, jnp.exp(masked - row_top[..., None]), 0.0)
    row_total = carried_share * prefix_total + jnp.sum(weights, axis=-1)
    summed = carried_share[..., None] * prefix_sum + jnp.einsum(
        "rhij,rjd->rhid",
        weights.astype(jnp.bfloat16),
        value_blocks,
        preferred_element_type=jnp.float32,
    )
    head_output = (summed / row_total[..., None]).astype(jnp.bfloat16)
    attended = head_output.transpose(0, 2, 1, 3).reshape(group_rows, query_width)
    attention_own = lax.psum_scatter(
        jnp.dot(attended, w_out, preferred_element_type=jnp.float32).astype(jnp.bfloat16),
        "mdl",
        scatter_dimension=0,
        tiled=True,
    ).astype(jnp.float32)
    residual = (tokens.astype(jnp.float32) + attention_own).astype(jnp.bfloat16)
    normed_mid = rms_scale(lax.all_gather(residual, "mdl", axis=0, tiled=True), feed_gain).astype(
        jnp.bfloat16
    )
    gate_value = jnp.dot(normed_mid, w_gate, preferred_element_type=jnp.float32)
    up_value = jnp.dot(normed_mid, w_up, preferred_element_type=jnp.float32)
    activation = (jax.nn.silu(gate_value) * up_value).astype(jnp.bfloat16)
    feed_own = lax.psum_scatter(
        jnp.dot(activation, w_down, preferred_element_type=jnp.float32).astype(jnp.bfloat16),
        "mdl",
        scatter_dimension=0,
        tiled=True,
    ).astype(jnp.float32)
    own_valid = lax.dynamic_slice_in_dim(valid_rows, model_place * local_rows, local_rows, 0)
    hidden = (
        (residual.astype(jnp.float32) + feed_own) * own_valid[:, None].astype(jnp.float32)
    ).astype(jnp.bfloat16)
    return (hidden, suffix_cache)


def any_specs(count):
    return [pl.BlockSpec(memory_space=pltpu.HBM)] * count


def device_call(kernel, outputs, in_specs, scratch, steps=1, out_specs=None, flops=2_000_000_000):
    return pl.pallas_call(
        kernel,
        out_shape=outputs,
        grid_spec=pltpu.PrefetchScalarGridSpec(
            num_scalar_prefetch=1,
            grid=(steps,),
            in_specs=in_specs,
            out_specs=out_specs
            or jax.tree.map(
                lambda out: pl.BlockSpec(out.shape, lambda *_: (0,) * len(out.shape)), outputs
            ),
            scratch_shapes=scratch,
        ),
        compiler_params=pltpu.CompilerParams(vmem_limit_bytes=60 * 1024 * 1024),
        cost_estimate=pl.CostEstimate(flops=flops, bytes_accessed=1, transcendentals=0),
    )


def whole_spec(array):
    return pl.BlockSpec(array.shape, lambda *_: (0,) * array.ndim)


def across_first(index, count):
    return [(place, place ^ index) for place in range(count)]


def dot_rows(left, right):
    return lax.dot_general(left, right, (((1,), (1,)), ((), ())), preferred_element_type=jnp.float32)


def square_first(block):
    return (
        lax.ppermute(block, "req", across_first(1, 4)),
        lax.ppermute(block, "req", across_first(2, 4)),
    )


def square_second(beside, above):
    half = beside.shape[0] // 2
    return (
        lax.ppermute(above[:half], "req", across_first(1, 4)),
        lax.ppermute(beside[half:], "req", across_first(2, 4)),
    )


def project_kernel(idx, rows, *refs):
    weight_refs = refs[:5]
    cosine_ref, sine_ref, query_ref, cache_ref, weights, sems = refs[5:]
    square = idx[2]
    full, depth = weights.shape[0], weight_refs[0].shape[1]
    half_out = weight_refs[3].shape[0]

    @pl.when(pl.program_id(0) == 0)
    def _():
        copies = []
        for number, (flip, start, size) in enumerate(
            [
                (0, 0, full),
                (1, 0, full),
                (2, 0, full),
                (3, 0, half_out),
                (3, half_out, full - half_out),
            ]
        ):
            columns = pl.ds(pl.multiple_of((square ^ flip) * depth, 128), depth)
            copies.append(
                pltpu.make_async_copy(
                    weight_refs[number].at[pl.ds(0, size), :],
                    weights.at[pl.ds(start, size), columns],
                    sems.at[number],
                )
            )
        for copy in copies:
            copy.start()
        for copy in copies:
            copy.wait()

    half = HD // 2
    length = idx[3 + square * pl.num_programs(0) + pl.program_id(0)]
    block = rows.shape[0] // 2
    for part in range(2):
        here = slice(part * block, (part + 1) * block)
        projected = dot_rows(weights[...], rows[here, :])
        cosine, sine = cosine_ref[:, here], sine_ref[:, here]

        def turned(start):
            lower, upper = projected[start : start + half], projected[start + half : start + HD]
            return jnp.concatenate(
                [lower * cosine - upper * sine, upper * cosine + lower * sine], axis=0
            )

        for head in range(2):
            query_ref[head, here, :] = turned(head * HD).T.astype(jnp.bfloat16)
        live = part * block + lax.broadcasted_iota(jnp.int32, (HD, block), 1) < length
        cache_ref[0, :, here] = jnp.where(live, turned(2 * HD), 0.0).astype(jnp.bfloat16)
        cache_ref[1, :, here] = jnp.where(live, projected[3 * HD :], 0.0).astype(jnp.bfloat16)


def attend_kernel(
    shift,
    lines,
    idx,
    query_all,
    cache_all,
    own,
    beside,
    above,
    far_key,
    far_value,
    same_ref,
    other_ref,
    queries,
    suffix,
    key_buf,
    value_buf,
    sems,
):
    line, core, square = idx[0], idx[1], idx[2]
    request = square * lines + lax.rem(line + shift, lines)
    requests = lines * 4
    length = idx[3 + request]
    source = idx[3 + 2 * requests + idx[3 + requests + request]] ^ square
    plen = key_buf.shape[1]
    tail = suffix.shape[2]
    rows = pl.ds(pl.multiple_of(lax.rem(line + shift, lines) * tail, 128), tail)
    own_copies = [
        pltpu.make_async_copy(query_all.at[:, rows, :], queries, sems.at[2]),
        pltpu.make_async_copy(cache_all.at[:, :, rows], suffix, sems.at[3]),
    ]
    for copy in own_copies:
        copy.start()
    keys = [own.at[0], beside.at[0], above.at[0], far_key.at[0]]
    values = [own.at[1], beside.at[1], above.at[1], far_value.at[0]]

    def prefix_copies(number):
        return [
            pltpu.make_async_copy(keys[number], key_buf, sems.at[0]),
            pltpu.make_async_copy(
                values[number], value_buf.at[pl.ds(0, HD), pl.ds(0, plen)], sems.at[1]
            ),
        ]

    for number in range(4):

        @pl.when(source == number)
        def _(number=number):
            for copy in prefix_copies(number):
                copy.start()

    value_buf[HD:, :] = (
        (lax.broadcasted_iota(jnp.int32, (value_buf.shape[0] - HD, plen + tail), 0) == 0)
        .astype(jnp.float32)
        .astype(jnp.bfloat16)
    )
    for copy in own_copies:
        copy.wait()
    value_buf[:HD, pl.ds(plen, tail)] = suffix[1]
    for copy in prefix_copies(0):
        copy.wait()
    factor = math.log2(math.e) / math.sqrt(HD)
    chunk = 512
    parts = plen // chunk + 1

    def one_block(start, rows, out_ref):
        pair = jnp.concatenate(
            [queries[0, pl.ds(start, rows), :], queries[1, pl.ds(start, rows), :]], axis=0
        )

        def score(part):
            if part < parts - 1:
                return jnp.dot(
                    pair,
                    key_buf[:, part * chunk : (part + 1) * chunk],
                    preferred_element_type=jnp.float32,
                )
            scores = jnp.dot(pair, suffix[0], preferred_element_type=jnp.float32)
            row = lax.broadcasted_iota(jnp.int32, scores.shape, 0)
            row = start + jnp.where(row >= rows, row - rows, row)
            column = lax.broadcasted_iota(jnp.int32, scores.shape, 1)
            allowed = jnp.logical_and(column <= row, column < length)
            return jnp.where(allowed, scores, far_below)

        top, total = None, None
        following = score(0)
        for part in range(parts):
            scores = following
            if part + 1 < parts:
                following = score(part + 1)
            size = scores.shape[1]
            held = value_buf[:, part * chunk : part * chunk + size]
            highest = jnp.max(scores, axis=1, keepdims=True)
            new_top = highest if top is None else jnp.maximum(top, highest)
            added = dot_rows(
                jnp.exp2((scores - new_top) * factor).astype(jnp.bfloat16), held
            )
            total = (
                added if total is None else total * jnp.exp2((top - new_top) * factor) + added
            )
            top = new_top
        result = (total[:, :HD] / total[:, HD : HD + 1]).astype(jnp.bfloat16)
        out_ref[:rows, :] = jnp.concatenate([result[:rows], result[rows:]], axis=1)

    halves = tail // 2
    for flip, out_ref in enumerate((same_ref, other_ref)):
        start = pl.multiple_of((core ^ flip) * halves, halves)

        @pl.when(start < length)
        def _(start=start, out_ref=out_ref):
            one_block(start, halves, out_ref)

        @pl.when(start >= length)
        def _(out_ref=out_ref):
            out_ref[...] = jnp.zeros(out_ref.shape, jnp.bfloat16)


def output_kernel(lines, idx, *refs):
    pieces = refs[: 2 * lines]
    out_refs, refs = refs[2 * lines : 2 * lines + 10], refs[2 * lines + 10 :]
    tokens, gain, residual_ref, normed_ref, weight, held, sems = refs
    line, core, square = idx[0], idx[1], idx[2]
    depth, width = held.shape[2], out_refs[0].shape[1]
    half = weight.shape[0] // 2
    copies = []
    for number, ref in enumerate(out_refs):
        flip = min(number % 5, 3)
        first = number // 5 * half + (half // 2 if number % 5 == 4 else 0)
        columns = pl.ds(pl.multiple_of((square ^ flip) * width, 128), width)
        target = weight.at[pl.ds(first, ref.shape[0]), columns]
        copies.append(pltpu.make_async_copy(ref, target, sems.at[len(pieces) + number]))
    copies += [
        pltpu.make_async_copy(piece, held.at[number], sems.at[number])
        for number, piece in enumerate(pieces)
    ]
    for copy in copies:
        copy.start()
    for copy in copies:
        copy.wait()
    total = jnp.zeros(tokens.shape, jnp.float32)
    for number in range(len(pieces)):
        shift, flip = number // 2, number % 2
        came = lax.rem(line + lines - shift, lines) ^ line
        place = flip * lines + (came >> 1) + (came & 1) * 2
        total += jnp.dot(
            held[number],
            weight[pl.ds(pl.multiple_of(place * depth, 16), depth), :],
            preferred_element_type=jnp.float32,
        )
    residual = (tokens[...].astype(jnp.float32) + total).astype(jnp.bfloat16)
    residual_ref[...] = residual
    numbers = residual.astype(jnp.float32)
    mean_square = jnp.mean(numbers * numbers, axis=-1, keepdims=True)
    normed_ref[...] = (
        numbers * lax.rsqrt(mean_square + norm_eps) * gain[...].astype(jnp.float32)
    ).astype(jnp.bfloat16)


def packed_copies(refs, square, first, size, target, sems):
    split = refs[3].shape[0]
    copies = []

    def add(ref, start, count, place, offset):
        rows = pl.ds(pl.multiple_of(place * size, 16) + offset, count)
        copies.append((ref.at[pl.ds(start, count), :], target.at[rows, :]))

    for flip in range(3):
        add(refs[flip], first, size, square ^ flip, 0)
    low = max(min(split - first, size), 0)
    if low:
        add(refs[3], first, low, square ^ 3, 0)
    if low < size:
        add(refs[4], max(first - split, 0), size - low, square ^ 3, low)
    return [
        pltpu.make_async_copy(source, place, sems.at[number])
        for number, (source, place) in enumerate(copies)
    ]


def activate_kernel(row_count, idx, *refs):
    weight_refs, row_refs = refs[:5], refs[5 : 5 + row_count]
    out_ref, gate, up, held, sems, row_sems = refs[5 + row_count :]
    size = gate.shape[0] // 4
    copies = packed_copies(weight_refs, idx[2], 0, size, gate, sems.at[0])
    copies += packed_copies(weight_refs, idx[2], size, size, up, sems.at[1])
    copies += [
        pltpu.make_async_copy(row_ref, held.at[number], row_sems.at[number])
        for number, row_ref in enumerate(row_refs)
    ]
    for copy in copies:
        copy.start()
    for copy in copies:
        copy.wait()
    block = row_refs[0].shape[0]
    for number in range(row_count):
        rows = held[number]
        gated = jnp.dot(rows, gate[...], preferred_element_type=jnp.float32)
        upper = jnp.dot(rows, up[...], preferred_element_type=jnp.float32)
        out_ref[number * block : (number + 1) * block, :] = (
            gated / (1.0 + jnp.exp(-gated)) * upper
        ).astype(jnp.bfloat16)


def down_kernel(block, idx, *refs):
    first_act, second_act, out_a, out_b, first, second, sems = refs[10:]
    size = first.shape[0] // 4
    copies = packed_copies(refs[:5], idx[2], 2 * size, size, first, sems.at[0])
    copies += packed_copies(refs[5:10], idx[2], 2 * size, size, second, sems.at[1])
    for copy in copies:
        copy.start()
    for copy in copies:
        copy.wait()
    for number, out_ref in enumerate((out_a, out_b)):
        here = slice(number * block, (number + 1) * block)
        out_ref[...] = (
            dot_rows(first_act[here], first[...]) + dot_rows(second_act[here], second[...])
        ).astype(jnp.bfloat16)


def square_local(
    tokens,
    attention_gain,
    feed_gain,
    w_query,
    w_key,
    w_value,
    w_out,
    w_gate,
    w_up,
    w_down,
    prefix_cache,
    lengths,
    member,
    owners,
):
    model_devices = lax.axis_size("mdl")
    lines = model_devices // 2
    place = lax.axis_index("mdl")
    square = lax.axis_index("req")
    line, core = place // 2, place % 2
    block, width = tokens.shape
    group_rows = block * model_devices
    hidden = w_gate.shape[1]
    plen = prefix_cache.shape[2]
    bf16 = jnp.bfloat16

    def to_core(array):
        return lax.ppermute(array, "mdl", across_first(1, model_devices))

    def to_line(array, flip):
        return lax.ppermute(array, "mdl", across_first(flip, model_devices))

    def shifted(array, step, flip):
        route = []
        for spot in range(lines):
            for side in range(2):
                route.append((2 * spot + side, 2 * ((spot + step) % lines) + (side ^ flip)))
        return lax.ppermute(array, "mdl", route)

    where_am_i = jnp.concatenate(
        [jnp.stack([line, core, square]).astype(jnp.int32), lengths, member, owners]
    )

    def after(arrays, *others):
        return lax.optimization_barrier((tuple(arrays), others))[0]

    normed = rms_scale(tokens, attention_gain).astype(bf16)
    group_normed = lax.all_gather(normed, "mdl", axis=0, tiled=True)
    projection = jnp.concatenate([w_query.T, w_key.T, w_value.T], axis=0)
    projection_near = square_first(projection)
    prefix = jnp.swapaxes(prefix_cache[:, 0], 1, 2)
    prefix_near = square_first(prefix)
    out_own = jnp.concatenate([w_out, to_line(w_out, 4)], axis=0)
    out_own = jnp.concatenate([out_own, to_line(out_own, 2)], axis=0)
    feed = jnp.concatenate([w_gate, w_up, w_down.T], axis=0)
    unit = feed.shape[0] // 12
    feed_parts = jnp.split(feed, [4 * unit, 7 * unit])
    feed_z = [to_line(feed_parts[0], 4)]

    *near, feed_part = after(
        [*projection_near, *prefix_near, feed_parts[1]],
        *projection_near,
        *prefix_near,
        out_own,
        *feed_z,
    )
    projection_near, prefix_near = near[:2], near[2:]
    projection_far = square_second(*projection_near)
    prefix_far = square_second(*prefix_near)
    feed_z.append(to_line(feed_part, 4))

    out_late, feed_part = after(
        [out_own, feed_parts[2]], *projection_far, *prefix_far, feed_z[1]
    )
    out_near = square_first(out_late)
    feed_z.append(to_line(feed_part, 4))

    half = HD // 2
    frequency = rope_base ** (-(jnp.arange(half).astype(jnp.float32) * 2.0 / HD))
    positions = (jnp.arange(SUF, dtype=jnp.int32) + plen).astype(jnp.float32)
    angles = frequency[:, None] * positions[None, :]
    cosine, sine = jnp.cos(angles), jnp.sin(angles)
    queries, cache = device_call(
        project_kernel,
        (
            jax.ShapeDtypeStruct((2, group_rows, HD), bf16),
            jax.ShapeDtypeStruct((2, HD, group_rows), bf16),
        ),
        [pl.BlockSpec((SUF, width), lambda step, *_: (step, 0))]
        + any_specs(5)
        + [whole_spec(cosine), whole_spec(sine)],
        [pltpu.VMEM((4 * HD, width), bf16), pltpu.SemaphoreType.DMA((5,))],
        lines,
        (
            pl.BlockSpec((2, SUF, HD), lambda step, *_: (0, step, 0)),
            pl.BlockSpec((2, HD, SUF), lambda step, *_: (0, 0, step)),
        ),
    )(
        where_am_i,
        *after([group_normed], *prefix_far, feed_z[1]),
        projection,
        *projection_near,
        *projection_far,
        cosine,
        sine,
    )

    *near, feed_late = after([*out_near, feed], queries)
    out_parts = [out_late, *out_near, *square_second(*near)]
    out_parts += [to_core(part) for part in out_parts]
    first_near = square_first(feed_late)

    pieces, done = {}, {}
    for shift in (2, 1, 3, 0):
        same, other = device_call(
            functools.partial(attend_kernel, shift, lines),
            (jax.ShapeDtypeStruct((SUF // 2, 2 * HD), bf16),) * 2,
            any_specs(7),
            [
                pltpu.VMEM((2, SUF, HD), bf16),
                pltpu.VMEM((2, HD, SUF), bf16),
                pltpu.VMEM((HD, plen), bf16),
                pltpu.VMEM((128, plen + SUF), bf16),
                pltpu.SemaphoreType.DMA((4,)),
            ],
            flops=5_000_000_000,
        )(where_am_i, queries, cache, prefix, *prefix_near, *prefix_far)
        done[shift] = same
        (queries,) = after([queries], same, feed_z[2], *pieces.get({1: 2, 3: 1}.get(shift), ()))
        if shift:
            pieces[shift] = (shifted(same, shift, 0), shifted(other, shift, 1))
        else:
            pieces[shift] = (same, to_core(other))

    first_far = square_second(*after(first_near, done[2]))
    first_feed = [feed_late, *first_near, *first_far]
    (feed_z,) = after([jnp.concatenate(feed_z, axis=0)], *first_far, done[3])
    second_near = square_first(feed_z)
    second_feed = [feed_z, *second_near, *square_second(*second_near)]
    attended = [piece for shift in range(lines) for piece in pieces[shift]]
    residual, normed_mid = device_call(
        functools.partial(output_kernel, lines),
        (jax.ShapeDtypeStruct((block, width), bf16),) * 2,
        any_specs(len(attended) + len(out_parts))
        + [whole_spec(tokens), pl.BlockSpec((1, width), lambda *_: (0, 0))],
        [
            pltpu.VMEM((width, width), bf16),
            pltpu.VMEM((len(attended), *attended[0].shape), bf16),
            pltpu.SemaphoreType.DMA((len(attended) + len(out_parts),)),
        ],
    )(where_am_i, *attended, *out_parts, tokens, feed_gain[None, :])

    def to_neighbour(array):
        return lax.ppermute(array, "mdl", across_first(2, model_devices))

    far_rows = to_neighbour(normed_mid)
    own_rows = [normed_mid, to_core(normed_mid)]
    far_rows = [far_rows, to_core(far_rows)]

    def activate(weights, rows):
        return device_call(
            functools.partial(activate_kernel, len(rows)),
            jax.ShapeDtypeStruct((len(rows) * block, hidden), bf16),
            any_specs(5 + len(rows)),
            [
                pltpu.VMEM((width, hidden), bf16),
                pltpu.VMEM((width, hidden), bf16),
                pltpu.VMEM((len(rows), block, width), bf16),
                pltpu.SemaphoreType.DMA((2, 5)),
                pltpu.SemaphoreType.DMA((len(rows),)),
            ],
        )(where_am_i, *weights, *rows)

    first_own = activate(first_feed, own_rows)
    first_distant = activate(first_feed, far_rows)
    second_distant = activate(second_feed, after(far_rows, first_own))

    def down(first_act, second_act):
        return device_call(
            functools.partial(down_kernel, block),
            (jax.ShapeDtypeStruct((block, width), bf16),) * 2,
            any_specs(10) + [whole_spec(first_act), whole_spec(second_act)],
            [
                pltpu.VMEM((width, hidden), bf16),
                pltpu.VMEM((width, hidden), bf16),
                pltpu.SemaphoreType.DMA((2, 5)),
            ],
        )(where_am_i, *first_feed, *second_feed, first_act, second_act)

    def added(left, right):
        return left.astype(jnp.float32) + right.astype(jnp.float32)

    far_sum, far_core = down(first_distant, second_distant)
    far_sum = added(far_sum, to_core(far_core)).astype(bf16)
    second_own = activate(second_feed, after(own_rows, far_sum))
    far_sum = to_neighbour(far_sum)
    own_sum, own_core = down(first_own, second_own)
    own_core = jnp.concatenate([to_core(part) for part in jnp.split(own_core, 4)], axis=0)
    feed_sum = added(own_sum, own_core) + far_sum.astype(jnp.float32)
    live = core * block + jnp.arange(block, dtype=jnp.int32) < lax.dynamic_index_in_dim(
        lengths, square * lines + line, 0, False
    )
    result = jnp.where(live[:, None], residual.astype(jnp.float32) + feed_sum, 0.0).astype(bf16)
    return (result, jnp.swapaxes(cache, 1, 2))


def solution(mesh):
    placed = (
        P(("req", "mdl"), None),
        P(),
        P(),
        P("req", "mdl"),
        P("req", "mdl"),
        P("req", "mdl"),
        P("mdl", "req"),
        P("req", "mdl"),
        P("req", "mdl"),
        P("mdl", "req"),
        P(None, "req", None, "mdl"),
        P(),
        P(),
        P(),
    )
    square = mesh.shape["req"] == 4 and mesh.shape["mdl"] == 8
    return jax.shard_map(
        square_local if square else local,
        mesh=mesh,
        in_specs=placed,
        out_specs=(P(("req", "mdl"), None), P(None, "req", "mdl")),
        check_vma=False,
    )
```

```python
import functools
import math

import jax
import jax.numpy as jnp
from jax import lax
from jax.experimental import pallas as pl
from jax.experimental.pallas import tpu as pltpu
from jax.sharding import PartitionSpec as P

HD = 96
SUF = 512


rope_base = 100000.0
norm_eps = 1e-05
far_below = -1e30


def from_partner(block, axis, bit):
    count = lax.axis_size(axis)
    route = []
    for low in range(count):
        high = low | 1 << bit
        if high != low and high < count:
            route += [(low, high), (high, low)]
    return lax.ppermute(block, axis, route)


def rms_scale(row_values, norm_gain):
    numbers = row_values.astype(jnp.float32)
    mean_square = jnp.mean(numbers * numbers, axis=-1, keepdims=True)
    return numbers * lax.rsqrt(mean_square + norm_eps) * norm_gain.astype(jnp.float32)


def rotate(numbers, positions):
    half_width = numbers.shape[-1] // 2
    frequency = rope_base ** (
        -(jnp.arange(half_width).astype(jnp.float32) * 2.0 / numbers.shape[-1])
    )
    angles = positions[:, None] * frequency[None, :]
    cosine = jnp.cos(angles)[:, None, :]
    sine_part = jnp.sin(angles)[:, None, :]
    lower_half = numbers[..., :half_width]
    upper_half = numbers[..., half_width:]
    return jnp.concatenate(
        [
            lower_half * cosine - upper_half * sine_part,
            upper_half * cosine + lower_half * sine_part,
        ],
        axis=-1,
    )


def prefix_part(query_block, key_rows, value_rows, score_scale):
    scores = (
        jnp.einsum("hid,jd->hij", query_block, key_rows, preferred_element_type=jnp.float32)
        * score_scale
    )
    row_top = jnp.max(scores, axis=-1)
    weights = jnp.exp(scores - row_top[..., None])
    row_total = jnp.sum(weights, axis=-1)
    summed = jnp.einsum(
        "hij,jd->hid", weights.astype(jnp.bfloat16), value_rows, preferred_element_type=jnp.float32
    )
    return (row_top, row_total, summed)


def local(
    tokens,
    attention_gain,
    feed_gain,
    w_query,
    w_key,
    w_value,
    w_out,
    w_gate,
    w_up,
    w_down,
    prefix_cache,
    lengths,
    member,
    owners,
):
    w_query, w_key, w_value, w_gate, w_up = (
        lax.all_gather(w_query, "req", axis=0, tiled=True),
        lax.all_gather(w_key, "req", axis=0, tiled=True),
        lax.all_gather(w_value, "req", axis=0, tiled=True),
        lax.all_gather(w_gate, "req", axis=0, tiled=True),
        lax.all_gather(w_up, "req", axis=0, tiled=True),
    )
    w_out, w_down = (
        lax.all_gather(w_out, "req", axis=1, tiled=True),
        lax.all_gather(w_down, "req", axis=1, tiled=True),
    )
    model_devices = lax.axis_size("mdl")
    model_place = lax.axis_index("mdl")
    group_place = lax.axis_index("req")
    local_rows = tokens.shape[0]
    group_rows = local_rows * model_devices
    local_requests = group_rows // SUF
    query_width = w_query.shape[1]
    heads_here = query_width // HD
    pair_width = w_key.shape[1]
    halves = HD // pair_width
    prefix_length = prefix_cache.shape[2]
    score_scale = 1.0 / math.sqrt(HD)
    stacked_weights = jnp.concatenate([w_query, w_key, w_value], axis=1)
    normed = rms_scale(lax.all_gather(tokens, "mdl", axis=0, tiled=True), attention_gain).astype(
        jnp.bfloat16
    )
    projected = jnp.dot(normed, stacked_weights, preferred_element_type=jnp.float32)
    projected_pair = jnp.stack(
        [
            projected[:, query_width : query_width + pair_width],
            projected[:, query_width + pair_width :],
        ],
        axis=0,
    )
    own_prefix = prefix_cache[:, 0]
    low_half = model_place % 2 == 0
    if halves > 1:
        partner = from_partner(projected_pair.astype(jnp.bfloat16), "mdl", 0).astype(
            projected_pair.dtype
        )
        full_pair = jnp.where(
            low_half,
            jnp.concatenate([projected_pair, partner], axis=2),
            jnp.concatenate([partner, projected_pair], axis=2),
        )
        prefix_partner = from_partner(own_prefix, "mdl", 0)
        prefix_full = jnp.where(
            low_half,
            jnp.concatenate([own_prefix, prefix_partner], axis=2),
            jnp.concatenate([prefix_partner, own_prefix], axis=2),
        )
    else:
        full_pair = projected_pair
        prefix_full = own_prefix
    offsets = jnp.arange(group_rows, dtype=jnp.int32) % SUF
    positions = (offsets + prefix_length).astype(jnp.float32)
    queries = rotate(
        projected[:, :query_width].reshape(group_rows, heads_here, HD), positions
    ).astype(jnp.bfloat16)
    keys_rotated = rotate(full_pair[0].reshape(group_rows, 1, HD), positions).reshape(
        group_rows, HD
    )
    key_rows = keys_rotated.astype(jnp.bfloat16)
    value_rows = full_pair[1].astype(jnp.bfloat16)
    local_lengths = lax.dynamic_slice_in_dim(lengths, group_place * local_requests, local_requests)
    valid = jnp.arange(SUF, dtype=jnp.int32)[None, :] < local_lengths[:, None]
    valid_rows = valid.reshape(group_rows)
    own_start = model_place % halves * pair_width
    key_own = lax.dynamic_slice_in_dim(keys_rotated, own_start, pair_width, 1)
    cache_rows = jnp.stack([key_own, projected_pair[1]], axis=0) * valid_rows[None, :, None].astype(
        jnp.float32
    )
    suffix_cache = cache_rows.astype(jnp.bfloat16)
    query_blocks = queries.reshape(local_requests, SUF, heads_here, HD).transpose(0, 2, 1, 3)
    group_numbers = jnp.arange(owners.shape[0], dtype=jnp.int32)
    every_prefix = lax.all_gather(prefix_full[:, None], "req", axis=1, tiled=True)
    local_members = lax.dynamic_slice_in_dim(member, group_place * local_requests, local_requests)
    slot_ids = jnp.sum(
        jnp.where(local_members[:, None] == group_numbers[None, :], owners[None, :], 0), axis=1
    )

    def attend(request):
        slot_index = slot_ids[request]
        prefix_keys = lax.dynamic_index_in_dim(every_prefix[0], slot_index, 0, keepdims=False)
        prefix_values = lax.dynamic_index_in_dim(every_prefix[1], slot_index, 0, keepdims=False)
        return prefix_part(query_blocks[request], prefix_keys, prefix_values, score_scale)

    prefix_top, prefix_total, prefix_sum = lax.map(
        attend, jnp.arange(local_requests, dtype=jnp.int32)
    )
    key_blocks = key_rows.reshape(local_requests, SUF, HD)
    value_blocks = value_rows.reshape(local_requests, SUF, HD)
    scores = (
        jnp.einsum("rhid,rjd->rhij", query_blocks, key_blocks, preferred_element_type=jnp.float32)
        * score_scale
    )
    causal = jnp.arange(SUF)[:, None] >= jnp.arange(SUF)[None, :]
    allowed = (causal[None, :, :] & valid[:, None, :])[:, None]
    masked = jnp.where(allowed, scores, far_below)
    row_top = jnp.maximum(prefix_top, jnp.max(masked, axis=-1))
    carried_share = jnp.exp(prefix_top - row_top)
    weights = jnp.where(allowed, jnp.exp(masked - row_top[..., None]), 0.0)
    row_total = carried_share * prefix_total + jnp.sum(weights, axis=-1)
    summed = carried_share[..., None] * prefix_sum + jnp.einsum(
        "rhij,rjd->rhid",
        weights.astype(jnp.bfloat16),
        value_blocks,
        preferred_element_type=jnp.float32,
    )
    head_output = (summed / row_total[..., None]).astype(jnp.bfloat16)
    attended = head_output.transpose(0, 2, 1, 3).reshape(group_rows, query_width)
    attention_own = lax.psum_scatter(
        jnp.dot(attended, w_out, preferred_element_type=jnp.float32).astype(jnp.bfloat16),
        "mdl",
        scatter_dimension=0,
        tiled=True,
    ).astype(jnp.float32)
    residual = (tokens.astype(jnp.float32) + attention_own).astype(jnp.bfloat16)
    normed_mid = rms_scale(lax.all_gather(residual, "mdl", axis=0, tiled=True), feed_gain).astype(
        jnp.bfloat16
    )
    gate_value = jnp.dot(normed_mid, w_gate, preferred_element_type=jnp.float32)
    up_value = jnp.dot(normed_mid, w_up, preferred_element_type=jnp.float32)
    activation = (jax.nn.silu(gate_value) * up_value).astype(jnp.bfloat16)
    feed_own = lax.psum_scatter(
        jnp.dot(activation, w_down, preferred_element_type=jnp.float32).astype(jnp.bfloat16),
        "mdl",
        scatter_dimension=0,
        tiled=True,
    ).astype(jnp.float32)
    own_valid = lax.dynamic_slice_in_dim(valid_rows, model_place * local_rows, local_rows, 0)
    hidden = (
        (residual.astype(jnp.float32) + feed_own) * own_valid[:, None].astype(jnp.float32)
    ).astype(jnp.bfloat16)
    return (hidden, suffix_cache)


def any_specs(count):
    return [pl.BlockSpec(memory_space=pl.ANY)] * count


def device_call(kernel, outputs, in_specs, scratch, steps=1, out_specs=None, flops=2_000_000_000):
    return pl.pallas_call(
        kernel,
        out_shape=outputs,
        grid_spec=pltpu.PrefetchScalarGridSpec(
            num_scalar_prefetch=1,
            grid=(steps,),
            in_specs=in_specs,
            out_specs=out_specs
            or jax.tree.map(
                lambda out: pl.BlockSpec(out.shape, lambda *_: (0,) * len(out.shape)), outputs
            ),
            scratch_shapes=scratch,
        ),
        compiler_params=pltpu.CompilerParams(vmem_limit_bytes=24 * 1024 * 1024),
        cost_estimate=pl.CostEstimate(flops=flops, bytes_accessed=1, transcendentals=0),
    )


def whole_spec(array):
    return pl.BlockSpec(array.shape, lambda *_: (0,) * array.ndim)


def across_first(index, count):
    return [(place, place ^ index) for place in range(count)]


def dot_rows(left, right):
    return lax.dot_general(left, right, (((1,), (1,)), ((), ())), preferred_element_type=jnp.float32)


def square_first(block):
    return (
        lax.ppermute(block, "req", across_first(1, 4)),
        lax.ppermute(block, "req", across_first(2, 4)),
    )


def square_second(beside, above):
    half = beside.shape[0] // 2
    return (
        lax.ppermute(above[:half], "req", across_first(1, 4)),
        lax.ppermute(beside[half:], "req", across_first(2, 4)),
    )


def project_kernel(idx, all_rows, *refs):
    weight_refs = refs[:5]
    cosine_ref, sine_ref, query_ref, cache_ref, weights, both_rows, sems, row_sems = refs[5:]
    square, step = idx[2], pl.program_id(0)
    size = both_rows.shape[1]

    def row_copy(number):
        slot = lax.rem(number, 2)
        place = pl.ds(pl.multiple_of(number * size, 128), size)
        return pltpu.make_async_copy(all_rows.at[place, :], both_rows.at[slot], row_sems.at[slot])

    full, depth = weights.shape[0], weight_refs[0].shape[1]
    half_out = weight_refs[3].shape[0]

    @pl.when(step == 0)
    def _():
        row_copy(step).start()
        copies = []
        for number, (flip, start, size) in enumerate(
            [
                (0, 0, full),
                (1, 0, full),
                (2, 0, full),
                (3, 0, half_out),
                (3, half_out, full - half_out),
            ]
        ):
            columns = pl.ds(pl.multiple_of((square ^ flip) * depth, 128), depth)
            copies.append(
                pltpu.make_async_copy(
                    weight_refs[number].at[pl.ds(0, size), :],
                    weights.at[pl.ds(start, size), columns],
                    sems.at[number],
                )
            )
        for copy in copies:
            copy.start()
        for copy in copies:
            copy.wait()

    pl.when(step + 1 < pl.num_programs(0))(lambda: row_copy(step + 1).start())
    row_copy(step).wait()
    rows = both_rows.at[lax.rem(step, 2)]
    half = HD // 2
    length = idx[3 + square * pl.num_programs(0) + step]
    block = size // 2
    for part in range(2):
        here = slice(part * block, (part + 1) * block)
        projected = dot_rows(weights[...], rows[here, :])
        cosine, sine = cosine_ref[:, here], sine_ref[:, here]

        def turned(start):
            lower, upper = projected[start : start + half], projected[start + half : start + HD]
            return jnp.concatenate(
                [lower * cosine - upper * sine, upper * cosine + lower * sine], axis=0
            )

        for head in range(2):
            query_ref[head, here, :] = turned(head * HD).T.astype(jnp.bfloat16)
        live = part * block + lax.broadcasted_iota(jnp.int32, (HD, block), 1) < length
        cache_ref[0, :, here] = jnp.where(live, turned(2 * HD), 0.0).astype(jnp.bfloat16)
        cache_ref[1, :, here] = jnp.where(live, projected[3 * HD :], 0.0).astype(jnp.bfloat16)


def attend_kernel(
    shift,
    lines,
    idx,
    query_all,
    cache_all,
    own,
    beside,
    above,
    far_key,
    far_value,
    same_ref,
    other_ref,
    queries,
    suffix,
    key_buf,
    value_buf,
    sems,
):
    line, core, square = idx[0], idx[1], idx[2]
    request = square * lines + lax.rem(line + shift, lines)
    requests = lines * 4
    length = idx[3 + request]
    source = idx[3 + 2 * requests + idx[3 + requests + request]] ^ square
    plen = key_buf.shape[1]
    tail = suffix.shape[2]
    rows = pl.ds(pl.multiple_of(lax.rem(line + shift, lines) * tail, 128), tail)
    own_copies = [
        pltpu.make_async_copy(query_all.at[:, rows, :], queries, sems.at[2]),
        pltpu.make_async_copy(cache_all.at[:, :, rows], suffix, sems.at[3]),
    ]
    for copy in own_copies:
        copy.start()
    keys = [own.at[0], beside.at[0], above.at[0], far_key.at[0]]
    values = [own.at[1], beside.at[1], above.at[1], far_value.at[0]]

    def prefix_copies(number):
        return [
            pltpu.make_async_copy(keys[number], key_buf, sems.at[0]),
            pltpu.make_async_copy(
                values[number], value_buf.at[pl.ds(0, HD), pl.ds(0, plen)], sems.at[1]
            ),
        ]

    for number in range(4):

        @pl.when(source == number)
        def _(number=number):
            for copy in prefix_copies(number):
                copy.start()

    value_buf[HD:, :] = (
        (lax.broadcasted_iota(jnp.int32, (value_buf.shape[0] - HD, plen + tail), 0) == 0)
        .astype(jnp.float32)
        .astype(jnp.bfloat16)
    )
    for copy in own_copies:
        copy.wait()
    value_buf[:HD, pl.ds(plen, tail)] = suffix[1]
    for copy in prefix_copies(0):
        copy.wait()
    factor = math.log2(math.e) / math.sqrt(HD)
    chunk = 512
    parts = plen // chunk + 1

    def one_block(start, rows, out_ref):
        pair = jnp.concatenate(
            [queries[0, pl.ds(start, rows), :], queries[1, pl.ds(start, rows), :]], axis=0
        )

        def score(part):
            if part < parts - 1:
                return jnp.dot(
                    pair,
                    key_buf[:, part * chunk : (part + 1) * chunk],
                    preferred_element_type=jnp.float32,
                )
            scores = jnp.dot(pair, suffix[0], preferred_element_type=jnp.float32)
            row = lax.broadcasted_iota(jnp.int32, scores.shape, 0)
            row = start + jnp.where(row >= rows, row - rows, row)
            column = lax.broadcasted_iota(jnp.int32, scores.shape, 1)
            allowed = jnp.logical_and(column <= row, column < length)
            return jnp.where(allowed, scores, far_below)

        top, total = None, None
        following = score(0)
        for part in range(parts):
            scores = following
            if part + 1 < parts:
                following = score(part + 1)
            size = scores.shape[1]
            held = value_buf[:, part * chunk : part * chunk + size]
            highest = jnp.max(scores, axis=1, keepdims=True)
            new_top = highest if top is None else jnp.maximum(top, highest)
            added = dot_rows(
                jnp.exp2((scores - new_top) * factor).astype(jnp.bfloat16), held
            )
            total = (
                added if total is None else total * jnp.exp2((top - new_top) * factor) + added
            )
            top = new_top
        result = (total[:, :HD] / total[:, HD : HD + 1]).astype(jnp.bfloat16)
        out_ref[:rows, :] = jnp.concatenate([result[:rows], result[rows:]], axis=1)

    halves = tail // 2
    for flip, out_ref in enumerate((same_ref, other_ref)):
        start = pl.multiple_of((core ^ flip) * halves, halves)

        @pl.when(start < length)
        def _(start=start, out_ref=out_ref):
            one_block(start, halves, out_ref)

        @pl.when(start >= length)
        def _(out_ref=out_ref):
            out_ref[...] = jnp.zeros(out_ref.shape, jnp.bfloat16)


def output_kernel(lines, idx, *refs):
    pieces = refs[: 2 * lines]
    out_refs, refs = refs[2 * lines : 2 * lines + 10], refs[2 * lines + 10 :]
    tokens, gain, residual_ref, normed_ref, weight, held, sems = refs
    line, core, square = idx[0], idx[1], idx[2]
    depth, width = held.shape[2], out_refs[0].shape[1]
    half = weight.shape[0] // 2
    copies = []
    for number, ref in enumerate(out_refs):
        flip = min(number % 5, 3)
        first = number // 5 * half + (half // 2 if number % 5 == 4 else 0)
        columns = pl.ds(pl.multiple_of((square ^ flip) * width, 128), width)
        target = weight.at[pl.ds(first, ref.shape[0]), columns]
        copies.append(pltpu.make_async_copy(ref, target, sems.at[len(pieces) + number]))
    copies += [
        pltpu.make_async_copy(piece, held.at[number], sems.at[number])
        for number, piece in enumerate(pieces)
    ]
    for copy in copies:
        copy.start()
    for copy in copies:
        copy.wait()
    total = jnp.zeros(tokens.shape, jnp.float32)
    for number in range(len(pieces)):
        shift, flip = number // 2, number % 2
        place = flip * lines + lax.rem(line + lines - shift, lines)
        total += jnp.dot(
            held[number],
            weight[pl.ds(pl.multiple_of(place * depth, 16), depth), :],
            preferred_element_type=jnp.float32,
        )
    residual = (tokens[...].astype(jnp.float32) + total).astype(jnp.bfloat16)
    residual_ref[...] = residual
    numbers = residual.astype(jnp.float32)
    mean_square = jnp.mean(numbers * numbers, axis=-1, keepdims=True)
    normed_ref[...] = (
        numbers * lax.rsqrt(mean_square + norm_eps) * gain[...].astype(jnp.float32)
    ).astype(jnp.bfloat16)


def packed_copies(refs, square, first, size, target, sems):
    split = refs[3].shape[0]
    copies = []

    def add(ref, start, count, place, offset):
        rows = pl.ds(pl.multiple_of(place * size, 16) + offset, count)
        copies.append((ref.at[pl.ds(start, count), :], target.at[rows, :]))

    for flip in range(3):
        add(refs[flip], first, size, square ^ flip, 0)
    low = max(min(split - first, size), 0)
    if low:
        add(refs[3], first, low, square ^ 3, 0)
    if low < size:
        add(refs[4], max(first - split, 0), size - low, square ^ 3, low)
    return [
        pltpu.make_async_copy(source, place, sems.at[number])
        for number, (source, place) in enumerate(copies)
    ]


def activate_kernel(row_count, idx, *refs):
    weight_refs, row_refs = refs[:5], refs[5 : 5 + row_count]
    out_ref, gate, up, held, sems, row_sems = refs[5 + row_count :]
    size = gate.shape[0] // 4
    copies = packed_copies(weight_refs, idx[2], 0, size, gate, sems.at[0])
    copies += packed_copies(weight_refs, idx[2], size, size, up, sems.at[1])
    copies += [
        pltpu.make_async_copy(row_ref, held.at[number], row_sems.at[number])
        for number, row_ref in enumerate(row_refs)
    ]
    for copy in copies:
        copy.start()
    for copy in copies:
        copy.wait()
    block = row_refs[0].shape[0]
    for number in range(row_count):
        rows = held[number]
        gated = jnp.dot(rows, gate[...], preferred_element_type=jnp.float32)
        upper = jnp.dot(rows, up[...], preferred_element_type=jnp.float32)
        out_ref[number * block : (number + 1) * block, :] = (
            gated / (1.0 + jnp.exp(-gated)) * upper
        ).astype(jnp.bfloat16)


def down_kernel(block, idx, *refs):
    first_act, second_act, out_a, out_b, first, second, sems = refs[10:]
    size = first.shape[0] // 4
    copies = packed_copies(refs[:5], idx[2], 2 * size, size, first, sems.at[0])
    copies += packed_copies(refs[5:10], idx[2], 2 * size, size, second, sems.at[1])
    for copy in copies:
        copy.start()
    for copy in copies:
        copy.wait()
    for number, out_ref in enumerate((out_a, out_b)):
        here = slice(number * block, (number + 1) * block)
        out_ref[...] = (
            dot_rows(first_act[here], first[...]) + dot_rows(second_act[here], second[...])
        ).astype(jnp.bfloat16)


def square_local(
    tokens,
    attention_gain,
    feed_gain,
    w_query,
    w_key,
    w_value,
    w_out,
    w_gate,
    w_up,
    w_down,
    prefix_cache,
    lengths,
    member,
    owners,
):
    model_devices = lax.axis_size("mdl")
    lines = model_devices // 2
    place = lax.axis_index("mdl")
    square = lax.axis_index("req")
    line, core = place // 2, place % 2
    block, width = tokens.shape
    group_rows = block * model_devices
    hidden = w_gate.shape[1]
    plen = prefix_cache.shape[2]
    bf16 = jnp.bfloat16

    def to_core(array):
        return lax.ppermute(array, "mdl", across_first(1, model_devices))

    def to_line(array, flip):
        return lax.ppermute(array, "mdl", across_first(flip, model_devices))

    def shifted(array, step, flip):
        route = []
        for spot in range(lines):
            for side in range(2):
                route.append((2 * spot + side, 2 * ((spot + step) % lines) + (side ^ flip)))
        return lax.ppermute(array, "mdl", route)

    where_am_i = jnp.concatenate(
        [jnp.stack([line, core, square]).astype(jnp.int32), lengths, member, owners]
    )

    def after(arrays, *others):
        return lax.optimization_barrier((tuple(arrays), others))[0]

    normed = rms_scale(tokens, attention_gain).astype(bf16)
    group_normed = lax.all_gather(normed, "mdl", axis=0, tiled=True)
    projection = jnp.concatenate([w_query.T, w_key.T, w_value.T], axis=0)
    projection_near = square_first(projection)
    prefix = jnp.swapaxes(prefix_cache[:, 0], 1, 2)
    prefix_near = square_first(prefix)
    out_own = lax.all_gather(
        w_out,
        "mdl",
        axis=0,
        tiled=True,
        axis_index_groups=[
            [2 * spot + side for spot in range(lines)] for side in range(2)
        ],
    )
    feed = jnp.concatenate([w_gate, w_up, w_down.T], axis=0)
    unit = feed.shape[0] // 72
    feed_parts = jnp.split(feed, [16 * unit, 28 * unit, 39 * unit, 50 * unit, 61 * unit])
    feed_z = [to_line(feed_parts[0], 4)]

    def send_next(*others):
        (part,) = after([feed_parts[len(feed_z)]], feed_z[-1], *others)
        feed_z.append(to_line(part, 4))
        return feed_z[-1]

    near = after(
        [*projection_near, *prefix_near], *projection_near, *prefix_near, *feed_z
    )
    projection_near, prefix_near = near[:2], near[2:]
    projection_far = square_second(*projection_near)
    prefix_far = square_second(*prefix_near)
    send_next(*near)

    (out_own,) = after([out_own], *projection_far, *prefix_far, feed_z[1])
    out_near = square_first(out_own)

    half = HD // 2
    frequency = rope_base ** (-(jnp.arange(half).astype(jnp.float32) * 2.0 / HD))
    positions = (jnp.arange(SUF, dtype=jnp.int32) + plen).astype(jnp.float32)
    angles = frequency[:, None] * positions[None, :]
    cosine, sine = jnp.cos(angles), jnp.sin(angles)
    queries, cache = device_call(
        project_kernel,
        (
            jax.ShapeDtypeStruct((2, group_rows, HD), bf16),
            jax.ShapeDtypeStruct((2, HD, group_rows), bf16),
        ),
        [pl.BlockSpec(memory_space=pltpu.HBM)] * 6
        + [whole_spec(cosine), whole_spec(sine)],
        [
            pltpu.VMEM((4 * HD, width), bf16),
            pltpu.VMEM((2, SUF, width), bf16),
            pltpu.SemaphoreType.DMA((5,)),
            pltpu.SemaphoreType.DMA((2,)),
        ],
        lines,
        (
            pl.BlockSpec((2, SUF, HD), lambda step, *_: (0, step, 0)),
            pl.BlockSpec((2, HD, SUF), lambda step, *_: (0, 0, step)),
        ),
    )(
        where_am_i,
        *after([group_normed], *prefix_far, feed_z[1]),
        projection,
        *projection_near,
        *projection_far,
        cosine,
        sine,
    )

    send_next(*prefix_far)
    *near, feed_late = after([*out_near, feed], queries)
    out_parts = [out_own, *out_near, *square_second(*near)]
    out_parts += [to_core(part) for part in out_parts]
    first_near = square_first(feed_late)
    (queries,) = after([queries], feed_z[-1])

    pieces, done = {}, {}
    for shift in (2, 1, 3, 0):
        same, other = device_call(
            functools.partial(attend_kernel, shift, lines),
            (jax.ShapeDtypeStruct((SUF // 2, 2 * HD), bf16),) * 2,
            any_specs(7),
            [
                pltpu.VMEM((2, SUF, HD), bf16),
                pltpu.VMEM((2, HD, SUF), bf16),
                pltpu.VMEM((HD, plen), bf16),
                pltpu.VMEM((128, plen + SUF), bf16),
                pltpu.SemaphoreType.DMA((4,)),
            ],
            flops=5_000_000_000,
        )(where_am_i, queries, cache, prefix, *prefix_near, *prefix_far)
        done[shift] = same
        if shift:
            came = {1: 2, 3: 1}.get(shift)
            (queries,) = after([queries], same, send_next(), *pieces.get(came, ()))
        if shift:
            pieces[shift] = (shifted(same, shift, 0), shifted(other, shift, 1))
        else:
            pieces[shift] = (same, to_core(other))

    first_far = square_second(*after(first_near, done[2]))
    first_feed = [feed_late, *first_near, *first_far]
    (feed_z,) = after([jnp.concatenate(feed_z, axis=0)], *first_far, done[3])
    second_near = square_first(feed_z)
    second_feed = [feed_z, *second_near, *square_second(*second_near)]
    attended = [piece for shift in range(lines) for piece in pieces[shift]]
    residual, normed_mid = device_call(
        functools.partial(output_kernel, lines),
        (jax.ShapeDtypeStruct((block, width), bf16),) * 2,
        any_specs(len(attended) + len(out_parts))
        + [whole_spec(tokens), pl.BlockSpec((1, width), lambda *_: (0, 0))],
        [
            pltpu.VMEM((width, width), bf16),
            pltpu.VMEM((len(attended), *attended[0].shape), bf16),
            pltpu.SemaphoreType.DMA((len(attended) + len(out_parts),)),
        ],
    )(where_am_i, *attended, *out_parts, tokens, feed_gain[None, :])

    def to_neighbour(array):
        return lax.ppermute(array, "mdl", across_first(2, model_devices))

    far_rows = to_neighbour(normed_mid)
    own_rows = [normed_mid, to_core(normed_mid)]
    far_rows = [far_rows, to_core(far_rows)]

    def activate(weights, rows):
        return device_call(
            functools.partial(activate_kernel, len(rows)),
            jax.ShapeDtypeStruct((len(rows) * block, hidden), bf16),
            any_specs(5 + len(rows)),
            [
                pltpu.VMEM((width, hidden), bf16),
                pltpu.VMEM((width, hidden), bf16),
                pltpu.VMEM((len(rows), block, width), bf16),
                pltpu.SemaphoreType.DMA((2, 5)),
                pltpu.SemaphoreType.DMA((len(rows),)),
            ],
        )(where_am_i, *weights, *rows)

    first_own = activate(first_feed, own_rows)
    far_rows = after(far_rows, first_own)
    first_distant = activate(first_feed, far_rows)
    second_distant = activate(second_feed, far_rows)

    def down(first_act, second_act):
        return device_call(
            functools.partial(down_kernel, block),
            (jax.ShapeDtypeStruct((block, width), bf16),) * 2,
            any_specs(10) + [whole_spec(first_act), whole_spec(second_act)],
            [
                pltpu.VMEM((width, hidden), bf16),
                pltpu.VMEM((width, hidden), bf16),
                pltpu.SemaphoreType.DMA((2, 5)),
            ],
        )(where_am_i, *first_feed, *second_feed, first_act, second_act)

    def added(left, right):
        return left.astype(jnp.float32) + right.astype(jnp.float32)

    far_sum, far_core = down(first_distant, second_distant)
    far_sum = added(far_sum, to_core(far_core)).astype(bf16)
    second_own = activate(second_feed, after(own_rows, far_sum))
    far_sum = to_neighbour(far_sum)
    own_sum, own_core = down(first_own, second_own)
    own_core = jnp.concatenate([to_core(part) for part in jnp.split(own_core, 4)], axis=0)
    feed_sum = added(own_sum, own_core) + far_sum.astype(jnp.float32)
    live = core * block + jnp.arange(block, dtype=jnp.int32) < lax.dynamic_index_in_dim(
        lengths, square * lines + line, 0, False
    )
    result = jnp.where(live[:, None], residual.astype(jnp.float32) + feed_sum, 0.0).astype(bf16)
    return (result, jnp.swapaxes(cache, 1, 2))


def solution(mesh):
    placed = (
        P(("req", "mdl"), None),
        P(),
        P(),
        P("req", "mdl"),
        P("req", "mdl"),
        P("req", "mdl"),
        P("mdl", "req"),
        P("req", "mdl"),
        P("req", "mdl"),
        P("mdl", "req"),
        P(None, "req", None, "mdl"),
        P(),
        P(),
        P(),
    )
    square = mesh.shape["req"] == 4 and mesh.shape["mdl"] == 8
    return jax.shard_map(
        square_local if square else local,
        mesh=mesh,
        in_specs=placed,
        out_specs=(P(("req", "mdl"), None), P(None, "req", "mdl")),
        check_vma=False,
    )
```
